32 devices in a mesh: op: 2 (over core), sec: 16 (over z, y, x).
Axes of the slice: x: 2, y: 2, z: 4, core: 2. Of those that a mesh axis runs over, the one named last changes fastest.
Arguments:
- psi: bfloat16 [3, 128, 256, 256], P(None, 'sec'), may hold values from -6 to 6
- left_ops: bfloat16 [8, 128, 256, 256], P('op', 'sec'), may hold values from -0.125 to 0.125
- right_ops: bfloat16 [8, 128, 256, 256], P('op', 'sec'), may hold values from -0.375 to 0.375
- shifts: int32 [8], P('op'), may hold values from -1 to 1
- active: int32 [8, 128], P('op', 'sec'), may hold values 0 or 1
Outputs:
- right_view: bfloat16 [3, 256, 128, 256], P(None, 'sec', None, 'op')
The draws below stay inside these ranges and needn't reach their ends.
All inputs are finite; a program needn't handle non-finite values. No bound on the sum of `active` on one device may be relied on, other than what follows from the above.
Results may differ from the reference program's by a relative error of at most 0.0049.
Values may be sent and summed in bfloat16 or wider, within the bound.
No kernel may reach another device: no remote copies, remote signals or barrier semaphores. Data moves between devices by JAX's collectives and lax.ppermute only.
A program may use at most 64 MiB of HBM per device.

```python
import jax
import jax.numpy as jnp
from jax import lax

BLK = 256
NVEC = 3
QMAX = 1
TERMS = 8
NSEC = 128


def with_ends(array, rng, least, high):
    dims = array.shape
    index_at = [jax.random.randint(jax.random.fold_in(rng, axis), (), 0, dims[axis]) for axis in range(len(dims))]
    array = array.at[tuple(index_at)].set(least)
    longest = dims.index(max(dims))
    index_at[longest] = (index_at[longest] + 1) % dims[longest]
    return array.at[tuple(index_at)].set(high)


def block_levels(rng, shape, pieces, low, high):
    factor_of = 1.0
    for axis_at, blocks in pieces:
        heights = jax.random.uniform(jax.random.fold_in(jax.random.fold_in(rng, 6), axis_at), (blocks,), jnp.float32, low / len(pieces), high / len(pieces))
        factor_of = factor_of * jnp.repeat(jnp.exp(heights), shape[axis_at] // blocks).reshape((-1,) + (1,) * (len(shape) - 1 - axis_at))
    return factor_of


def centred(stream_key, dims, deviation, limit, split=(), held_as=jnp.bfloat16):
    level = block_levels(stream_key, dims, split, -0.22, 0.18) if split else 1.0
    values = jax.random.normal(stream_key, dims, jnp.float32) * deviation * level
    return jnp.minimum(jnp.maximum(values, -limit), limit).astype(held_as)


def setup_inputs(seed: int = 0) -> dict:
    splits = jax.random.split(jax.random.key(seed), 6)
    return {
        "psi": centred(splits[0], (NVEC, NSEC, BLK, BLK), 1.0, 6.0, ((1, 16),)),
        "left_ops": centred(splits[1], (TERMS, NSEC, BLK, BLK), (BLK * TERMS) ** -0.5, 0.125, ((0, 2), (1, 16))),
        "right_ops": centred(splits[2], (TERMS, NSEC, BLK, BLK), BLK ** -0.5, 0.375, ((0, 2), (1, 16))),
        "shifts": with_ends(jax.random.randint(splits[3], (TERMS,), 0 - QMAX, QMAX + 1), jax.random.fold_in(splits[3], 1), 0 - QMAX, QMAX).astype(jnp.int32),
        "active": with_ends((jax.random.randint(splits[4], (TERMS, NSEC), 0, 4) < 3).astype(jnp.int32), jax.random.fold_in(splits[4], 1), 0, 1),
    }


def reference(psi, left_ops, right_ops, shifts, active):
    sectors = jnp.arange(NSEC, dtype=jnp.int32)

    def step(total, items):
        left, right, shift, mask = items
        anchor = (sectors - shift).astype(jnp.int32)
        valid = (anchor >= 0) & (anchor < NSEC)
        picked = jnp.take(psi, jnp.clip(anchor, 0, NSEC - 1).astype(jnp.int32), axis=1).astype(jnp.float32)
        source = jnp.where(valid[None, :, None, None], picked, jnp.float32(0.0))
        middle = jnp.einsum("tij,vtjk->vtik", left.astype(jnp.float32), source).astype(jnp.bfloat16)
        middle = lax.optimization_barrier(middle).astype(jnp.float32)
        term = jnp.einsum("vtik,tlk->vlti", middle, right.astype(jnp.float32))
        weight = mask.astype(jnp.float32)
        return total + term * weight[None, None, :, None], None

    start = jnp.zeros((NVEC, BLK, NSEC, BLK), jnp.float32)
    total, _ = lax.scan(step, start, (left_ops, right_ops, shifts, active))
    return total.astype(jnp.bfloat16)
```

```python
import functools

import jax
import jax.numpy as jnp
from jax import lax
from jax.experimental import pallas as pl
from jax.experimental.pallas import tpu as pltpu
from jax.sharding import PartitionSpec as P

QMAX = 1
F32, B16 = jnp.float32, jnp.bfloat16


def neighbours(value):
    size, length = lax.axis_size("sec"), value.shape[1]
    up = [(i, i + 1) for i in range(size - 1)]
    down = [(j, i) for i, j in up]
    before = lax.ppermute(lax.slice_in_dim(value, length - QMAX, length, axis=1), "sec", up)
    after = lax.ppermute(lax.slice_in_dim(value, 0, QMAX, axis=1), "sec", down)
    return before, after


def products_kernel(me_ref, shifts_ref, active_ref, psi, before, after, left, right, mine, theirs,
                    ext, lbuf, rbuf, acc, mbuf, tbuf, sem_p, sem_l, sem_r, sem_o):
    nvec = psi.shape[0]
    count, sectors, blk, _ = left.shape
    half = blk // 2

    def load_psi():
        return [
            pltpu.make_async_copy(psi, ext.at[:, pl.ds(QMAX, sectors)], sem_p.at[0]),
            pltpu.make_async_copy(before, ext.at[:, pl.ds(0, QMAX)], sem_p.at[1]),
            pltpu.make_async_copy(after, ext.at[:, pl.ds(sectors + QMAX, QMAX)], sem_p.at[2]),
        ]

    def load_left(t):
        return pltpu.make_async_copy(left.at[:, pl.ds(t, 1)], lbuf.at[:, pl.ds(t, 1)], sem_l.at[t])

    def load_right(t):
        return pltpu.make_async_copy(right.at[:, pl.ds(t, 1)], rbuf.at[:, pl.ds(t, 1)], sem_r.at[t])

    for copy in load_psi():
        copy.start()
    for t in range(sectors):
        load_left(t).start()
        load_right(t).start()
    for copy in load_psi():
        copy.wait()

    def sector(t, carry):
        load_left(t).wait()
        load_right(t).wait()
        for v in range(nvec):
            middles = []
            for k in range(count):
                source = ext[v, t + QMAX - shifts_ref[k]]
                middle = jnp.dot(lbuf[k, t], source, preferred_element_type=F32)
                middles.append((middle * active_ref[k, t].astype(F32)).astype(B16))
            rights = jnp.concatenate([rbuf[k, t] for k in range(count)], axis=1)
            total = lax.dot_general(
                rights, jnp.concatenate(middles, axis=1), (((1,), (1,)), ((), ())), preferred_element_type=F32
            )
            for h in range(2):
                acc[v, h, pl.ds(t, blk, stride=sectors), :] = total[:, h * half : (h + 1) * half]
        return carry

    lax.fori_loop(0, sectors, sector, 0)
    me = me_ref[0]
    stores = []
    for v in range(nvec):
        tbuf[v] = acc[v, 1 - me].astype(B16)
        stores.append(pltpu.make_async_copy(tbuf.at[v], theirs.at[v], sem_o.at[0, v]))
        stores[-1].start()
        mbuf[v] = acc[v, me].astype(B16)
        stores.append(pltpu.make_async_copy(mbuf.at[v], mine.at[v], sem_o.at[1, v]))
        stores[-1].start()
    for copy in stores:
        copy.wait()


def products(me, shifts, active, psi, before, after, left, right):
    nvec = psi.shape[0]
    count, sectors, blk, _ = left.shape
    rows, half = blk * sectors, blk // 2
    smem = pl.BlockSpec(memory_space=pltpu.SMEM)
    hbm = pl.BlockSpec(memory_space=pl.ANY)
    out = jax.ShapeDtypeStruct((nvec, rows, half), B16)
    return pl.pallas_call(
        products_kernel,
        out_shape=(out, out),
        in_specs=[smem] * 3 + [hbm] * 5,
        out_specs=(hbm, hbm),
        scratch_shapes=[
            pltpu.VMEM((nvec, sectors + 2 * QMAX, blk, blk), B16),
            pltpu.VMEM((count, sectors, blk, blk), B16),
            pltpu.VMEM((count, sectors, blk, blk), B16),
            pltpu.VMEM((nvec, 2, rows, half), F32),
            pltpu.VMEM((nvec, rows, half), B16),
            pltpu.VMEM((nvec, rows, half), B16),
            pltpu.SemaphoreType.DMA((3,)),
            pltpu.SemaphoreType.DMA((sectors,)),
            pltpu.SemaphoreType.DMA((sectors,)),
            pltpu.SemaphoreType.DMA((2, nvec)),
        ],
        compiler_params=pltpu.CompilerParams(vmem_limit_bytes=48 * 2**20),
        cost_estimate=pl.CostEstimate(
            flops=4 * count * sectors * nvec * blk**3, bytes_accessed=16 * 2**20, transcendentals=0
        ),
        name="products",
    )(me, shifts, active, psi, before, after, left, right)


def general(psi, left_ops, right_ops, shifts, active):
    before, after = neighbours(psi)
    padded = jnp.concatenate([before, psi, after], axis=1)
    count = left_ops.shape[0]
    nvec, sectors, blk, _ = psi.shape

    def add_term(index, total):
        source = lax.dynamic_slice_in_dim(padded, QMAX - shifts[index], sectors, 1)
        middle = jnp.einsum("tij,vtjk->vtik", left_ops[index], source, preferred_element_type=F32).astype(B16)
        term = jnp.einsum("vtik,tlk->vlti", middle, right_ops[index], preferred_element_type=F32)
        weight = active[index].astype(F32)
        return total + term * weight[None, None, :, None]

    total = lax.fori_loop(0, count, add_term, jnp.zeros((nvec, blk, sectors, blk), F32))
    summed = lax.psum(total, "op")
    share = blk // lax.axis_size("op")
    owned = lax.dynamic_slice_in_dim(summed, lax.axis_index("op") * share, share, 3)
    return lax.all_to_all(owned.astype(B16), "sec", split_axis=1, concat_axis=2, tiled=True)


def per_device(psi, left_ops, right_ops, shifts, active):
    if lax.axis_size("op") != 2:
        return general(psi, left_ops, right_ops, shifts, active)
    nvec, sectors, blk, _ = psi.shape
    before, after = neighbours(psi)
    me = lax.axis_index("op").reshape(1)
    mine, theirs = products(me, shifts, active, psi, before, after, left_ops, right_ops)
    other = lax.ppermute(theirs, "op", [(0, 1), (1, 0)])
    owned = (mine.astype(F32) + other.astype(F32)).astype(B16)
    owned = owned.reshape(nvec, blk, sectors, blk // 2)
    return lax.all_to_all(owned, "sec", split_axis=1, concat_axis=2, tiled=True)


def solution(mesh):
    placed = (
        P(None, "sec", None, None),
        P("op", "sec", None, None),
        P("op", "sec", None, None),
        P("op"),
        P("op", "sec"),
    )
    return jax.shard_map(
        per_device,
        mesh=mesh,
        in_specs=placed,
        out_specs=P(None, "sec", None, "op"),
        check_vma=False,
    )
```

```python
import functools

import jax
import jax.numpy as jnp
from jax import lax
from jax.experimental import pallas as pl
from jax.experimental.pallas import tpu as pltpu
from jax.sharding import PartitionSpec as P

QMAX = 1
F32, B16 = jnp.float32, jnp.bfloat16


def neighbours(value, width):
    size, length = lax.axis_size("sec"), value.shape[1]
    up = [(i, i + 1) for i in range(size - 1)]
    down = [(j, i) for i, j in up]
    before = lax.ppermute(lax.slice_in_dim(value, length - width, length, axis=1), "sec", up)
    after = lax.ppermute(lax.slice_in_dim(value, 0, width, axis=1), "sec", down)
    return before, after


def fetch(psi, me):
    size, sectors = lax.axis_size("sec"), psi.shape[1]
    ahead = [(i, i + 1) for i in range(size - 1)]
    back = [(size + j, size + i) for i, j in ahead]
    part = lax.dynamic_slice_in_dim(psi, (1 - me) * (sectors - QMAX), QMAX, axis=1)
    return lax.ppermute(part, ("op", "sec"), ahead + back)


def swap(value):
    return lax.ppermute(value, "op", [(0, 1), (1, 0)])


def plan(nvec, sectors, early):
    inner = range(QMAX, sectors - QMAX)
    edge = [*range(QMAX), *range(sectors - QMAX, sectors)]
    first = [(v, t) for t in inner for v in range(early)]
    inside = [(v, t) for t in inner for v in range(early, nvec)]
    border = [(v, t) for t in edge for v in range(nvec)]
    return first, inside, border


class Work:
    def __init__(self, refs, psi, left, right, shifts, active, me, vectors):
        self.ext, self.lbuf, self.rbuf, self.obuf, self.sem_p, self.sem_l, self.sem_r, self.sem_o = refs
        self.psi, self.left, self.right, self.shifts, self.active, self.me = psi, left, right, shifts, active, me
        self.vectors = pl.ds(vectors[0], len(vectors)) if vectors else None
        self.sectors = left.shape[1]

    def operators(self, t):
        one = pl.ds(t, 1)
        return [
            pltpu.make_async_copy(self.left.at[:, one], self.lbuf.at[:, one], self.sem_l.at[t]),
            pltpu.make_async_copy(self.right.at[:, one], self.rbuf.at[:, one], self.sem_r.at[t]),
        ]

    def source(self, s):
        return [
            pltpu.make_async_copy(
                self.psi.at[self.vectors, pl.ds(s, 1)], self.ext.at[self.vectors, pl.ds(s + QMAX, 1)], self.sem_p.at[s]
            )
        ]

    def stores(self, job, mine, theirs):
        return [
            pltpu.make_async_copy(self.obuf.at[self.me, job], mine.at[job], self.sem_o.at[0, job]),
            pltpu.make_async_copy(self.obuf.at[1 - self.me, job], theirs.at[job], self.sem_o.at[1, job]),
        ]

    def product(self, v, t, job):
        count, _, _, blk = self.left.shape
        half = blk // 2
        middles = []
        for k in range(count):
            source = self.ext[v, t + QMAX - self.shifts[k]]
            middle = jnp.dot(self.lbuf[k, t], source, preferred_element_type=F32)
            middles.append((middle * self.active[k, t].astype(F32)).astype(B16))
        rights = jnp.concatenate([self.rbuf[k, t] for k in range(count)], axis=1)
        total = lax.dot_general(
            rights, jnp.concatenate(middles, axis=1), (((1,), (1,)), ((), ())), preferred_element_type=F32
        )
        for h in range(2):
            self.obuf[h, job] = total[:, h * half : (h + 1) * half].astype(B16)

    def start_inner(self):
        for s in range(2 * QMAX):
            for copy in self.source(s):
                copy.start()
        for t in range(QMAX, self.sectors - QMAX):
            for copy in self.source(t + QMAX) + self.operators(t):
                copy.start()

    def inner(self, vectors, group, mine, theirs):
        for s in range(2 * QMAX):
            for copy in self.source(s):
                copy.wait()

        def body(index, carry):
            at = [QMAX + index * group + place for place in range(group)]
            for t in at:
                for copy in self.source(t + QMAX) + self.operators(t):
                    copy.wait()
            self.several([(v, t) for t in at for v in vectors], index * group * len(vectors), mine, theirs)
            return carry

        lax.fori_loop(0, (self.sectors - 2 * QMAX) // group, body, 0)

    def several(self, jobs, base, mine, theirs):
        for place, (v, t) in enumerate(jobs):
            self.product(v, t, base + place)
        for place in range(len(jobs)):
            for copy in self.stores(base + place, mine, theirs):
                copy.start()

    def finish(self, jobs, mine, theirs):
        def body(job, carry):
            for copy in self.stores(job, mine, theirs):
                copy.wait()
            return carry

        lax.fori_loop(0, jobs, body, 0)


def first_kernel(early, me_ref, shifts, active, psi, left, right, mine, theirs, *refs):
    work = Work(refs, psi, left, right, shifts, active, me_ref[0], range(early))
    work.start_inner()
    work.inner(range(early), 2, mine, theirs)
    work.finish(mine.shape[0], mine, theirs)


def second_kernel(early, me_ref, shifts, active, psi, left, right, halo, other, mine, theirs, *refs):
    nvec, sectors = psi.shape[:2]
    me = me_ref[0]
    late = range(early, nvec)
    *refs, sem_h = refs
    work = Work(refs, psi, left, right, shifts, active, me, late)
    sides = []
    for index, at in enumerate((0, sectors - 2 * QMAX)):
        sides.append(
            pltpu.make_async_copy(
                psi.at[pl.ds(0, early), pl.ds(at, 2 * QMAX)],
                work.ext.at[pl.ds(0, early), pl.ds(at + QMAX, 2 * QMAX)],
                sem_h.at[index],
            )
        )
    for index, (source, core) in enumerate(((halo, me), (other, 1 - me))):
        at = core * (sectors + QMAX)
        sides.append(pltpu.make_async_copy(source, work.ext.at[:, pl.ds(at, QMAX)], sem_h.at[2 + index]))
    edge = [*range(QMAX), *range(sectors - QMAX, sectors)]
    if late:
        work.start_inner()
    for copy in sides:
        copy.start()
    for t in edge:
        for copy in work.operators(t):
            copy.start()
    if late:
        work.inner(late, 3, mine, theirs)
    for copy in sides:
        copy.wait()
    base = len(late) * (sectors - 2 * QMAX)
    for t in edge:
        for copy in work.operators(t):
            copy.wait()
        work.several([(v, t) for v in range(nvec)], base, mine, theirs)
        base += nvec
    work.finish(mine.shape[0], mine, theirs)


def products(kernel, early, jobs, vectors, me, shifts, active, psi, left, right, *more):
    count, sectors, blk, _ = left.shape
    half = blk // 2
    smem = pl.BlockSpec(memory_space=pltpu.SMEM)
    hbm = pl.BlockSpec(memory_space=pl.ANY)
    out = jax.ShapeDtypeStruct((jobs, blk, half), B16)
    return pl.pallas_call(
        functools.partial(kernel, early),
        out_shape=(out, out),
        in_specs=[smem] * 3 + [hbm] * 3 + [hbm] * len(more),
        out_specs=(hbm, hbm),
        scratch_shapes=[
            pltpu.VMEM((vectors, sectors + 2 * QMAX, blk, blk), B16),
            pltpu.VMEM((count, sectors, blk, blk), B16),
            pltpu.VMEM((count, sectors, blk, blk), B16),
            pltpu.VMEM((2, jobs, blk, half), B16),
            pltpu.SemaphoreType.DMA((sectors,)),
            pltpu.SemaphoreType.DMA((sectors,)),
            pltpu.SemaphoreType.DMA((sectors,)),
            pltpu.SemaphoreType.DMA((2, jobs)),
        ]
        + ([pltpu.SemaphoreType.DMA((4,))] if more else []),
        compiler_params=pltpu.CompilerParams(vmem_limit_bytes=60 * 2**20),
        cost_estimate=pl.CostEstimate(flops=2 * jobs * 2 * count * blk**3, bytes_accessed=12 * 2**20, transcendentals=0),
        name=kernel.__name__,
    )(me, shifts, active, psi, left, right, *more)


def combine_kernel(parts, behind, *refs):
    pairs, refs = refs[: 2 * parts], refs[2 * parts + behind :]
    owned, bufs, (obuf, sem) = refs[0], refs[1:-2], refs[-2:]
    size, _, share, half = obuf.shape
    loads = [pltpu.make_async_copy(ref, buf, sem.at[index]) for index, (ref, buf) in enumerate(zip(pairs, bufs))]
    for copy in loads:
        copy.start()
    base = 0
    for part in range(parts):
        loads[2 * part].wait()
        loads[2 * part + 1].wait()
        abuf, bbuf = bufs[2 * part], bufs[2 * part + 1]
        for job in range(abuf.shape[0]):
            total = (abuf[job].astype(F32) + bbuf[job].astype(F32)).astype(B16)
            obuf[:, base + job] = total.reshape(size, share, half)
        base += abuf.shape[0]
    store = pltpu.make_async_copy(obuf, owned, sem.at[0])
    store.start()
    store.wait()


def combine(pairs, size, *behind):
    refs = [ref for pair in pairs for ref in pair]
    jobs = sum(mine.shape[0] for mine, _ in pairs)
    _, blk, half = refs[0].shape
    hbm = pl.BlockSpec(memory_space=pl.ANY)
    block = (size, jobs, blk // size, half)
    return pl.pallas_call(
        functools.partial(combine_kernel, len(pairs), len(behind)),
        out_shape=jax.ShapeDtypeStruct(block, B16),
        in_specs=[hbm] * (len(refs) + len(behind)),
        out_specs=hbm,
        scratch_shapes=[pltpu.VMEM(ref.shape, B16) for ref in refs]
        + [pltpu.VMEM(block, B16), pltpu.SemaphoreType.DMA((len(refs),))],
        compiler_params=pltpu.CompilerParams(vmem_limit_bytes=16 * 2**20),
        cost_estimate=pl.CostEstimate(flops=0, bytes_accessed=0, transcendentals=0),
        name="combine",
    )(*refs, *behind)


def arrange_kernel(plans, sectors, *refs):
    count = len(plans)
    views, out, bufs, (acc, obuf, sem) = refs[:count], refs[count], refs[count + 1 : 2 * count + 1], refs[2 * count + 1 :]
    size, _, share, _ = bufs[0].shape
    loads = [pltpu.make_async_copy(view, buf, sem.at[index]) for index, (view, buf) in enumerate(zip(views, bufs))]
    for copy in loads:
        copy.start()
    for copy in loads:
        copy.wait()

    def body(source, carry):
        for buf, jobs in zip(bufs, plans):
            for job, (v, t) in enumerate(jobs):
                acc[v, pl.ds(source * sectors + t, share, stride=size * sectors), :] = buf[source, job].astype(F32)
        return carry

    lax.fori_loop(0, size, body, 0)
    stores = []
    for v in range(obuf.shape[0]):
        obuf[v] = acc[v].astype(B16)
        stores.append(pltpu.make_async_copy(obuf.at[v], out.at[v], sem.at[count + v]))
        stores[-1].start()
    for copy in stores:
        copy.wait()


def arrange(plans, views, nvec, sectors):
    size, _, share, half = views[0].shape
    rows = share * size * sectors
    hbm = pl.BlockSpec(memory_space=pl.ANY)
    out = pl.pallas_call(
        functools.partial(arrange_kernel, plans, sectors),
        out_shape=jax.ShapeDtypeStruct((nvec, rows, half), B16),
        in_specs=[hbm] * len(views),
        out_specs=hbm,
        scratch_shapes=[pltpu.VMEM(view.shape, B16) for view in views]
        + [
            pltpu.VMEM((nvec, rows, half), F32),
            pltpu.VMEM((nvec, rows, half), B16),
            pltpu.SemaphoreType.DMA((len(views) + nvec,)),
        ],
        compiler_params=pltpu.CompilerParams(vmem_limit_bytes=24 * 2**20),
        name="arrange",
    )(*views)
    return out.reshape(nvec, share, size * sectors, half)


def general(psi, left_ops, right_ops, shifts, active):
    before, after = neighbours(psi, QMAX)
    padded = jnp.concatenate([before, psi, after], axis=1)
    count = left_ops.shape[0]
    nvec, sectors, blk, _ = psi.shape

    def add_term(index, total):
        source = lax.dynamic_slice_in_dim(padded, QMAX - shifts[index], sectors, 1)
        middle = jnp.einsum("tij,vtjk->vtik", left_ops[index], source, preferred_element_type=F32).astype(B16)
        term = jnp.einsum("vtik,tlk->vlti", middle, right_ops[index], preferred_element_type=F32)
        weight = active[index].astype(F32)
        return total + term * weight[None, None, :, None]

    total = lax.fori_loop(0, count, add_term, jnp.zeros((nvec, blk, sectors, blk), F32))
    summed = lax.psum(total, "op")
    share = blk // lax.axis_size("op")
    owned = lax.dynamic_slice_in_dim(summed, lax.axis_index("op") * share, share, 3)
    return lax.all_to_all(owned.astype(B16), "sec", split_axis=1, concat_axis=2, tiled=True)


def per_device(psi, left_ops, right_ops, shifts, active):
    nvec, sectors, blk, _ = psi.shape
    size, half = lax.axis_size("sec"), blk // 2
    if lax.axis_size("op") != 2 or sectors <= 2 * QMAX or blk % (16 * size):
        return general(psi, left_ops, right_ops, shifts, active)
    me = lax.axis_index("op")
    state = (me.reshape(1), shifts, active, psi, left_ops, right_ops)
    early = 2
    first, inside, border = plan(nvec, sectors, early)
    rest = inside + border

    def fence(make, jobs, *operands):
        zeros = lambda *_: (jnp.zeros((len(jobs), blk, half), B16),) * 2
        return lax.cond(shifts[0] <= QMAX, make, zeros, *operands)

    def begin(*state):
        mine, theirs = products(first_kernel, early, len(first), early, *state)
        return mine, swap(theirs)

    def go_on(*state):
        mine, theirs = products(second_kernel, early, len(rest), nvec, *state)
        return mine, swap(theirs)

    halo = fetch(psi, me)
    owned = combine([fence(begin, first, *state)], size, halo)
    views = [lax.all_to_all(owned, "sec", split_axis=0, concat_axis=0, tiled=True)]
    pair = fence(go_on, rest, *state, halo, swap(halo))
    owned = combine([pair], size, views[0])
    views.append(lax.all_to_all(owned, "sec", split_axis=0, concat_axis=0, tiled=True))
    return arrange([first, rest], views, nvec, sectors)


def solution(mesh):
    placed = (
        P(None, "sec", None, None),
        P("op", "sec", None, None),
        P("op", "sec", None, None),
        P("op"),
        P("op", "sec"),
    )
    return jax.shard_map(
        per_device,
        mesh=mesh,
        in_specs=placed,
        out_specs=P(None, "sec", None, "op"),
        check_vma=False,
    )
```

```python
import functools

import jax
import jax.numpy as jnp
from jax import lax
from jax.experimental import pallas as pl
from jax.experimental.pallas import tpu as pltpu
from jax.sharding import PartitionSpec as P

QMAX = 1
F32, B16 = jnp.float32, jnp.bfloat16


def neighbours(value, width):
    size, length = lax.axis_size("sec"), value.shape[1]
    up = [(i, i + 1) for i in range(size - 1)]
    down = [(j, i) for i, j in up]
    before = lax.ppermute(lax.slice_in_dim(value, length - width, length, axis=1), "sec", up)
    after = lax.ppermute(lax.slice_in_dim(value, 0, width, axis=1), "sec", down)
    return before, after


def fetch(psi, me):
    size, sectors = lax.axis_size("sec"), psi.shape[1]
    ahead = [(i, i + 1) for i in range(size - 1)]
    back = [(size + j, size + i) for i, j in ahead]
    turns = [(size - 1, 2 * size - 1), (size, 0)]
    part = lax.dynamic_slice_in_dim(psi, (1 - me) * (sectors - QMAX), QMAX, axis=1)
    return lax.ppermute(part, ("op", "sec"), ahead + turns + back)


def swap(value):
    return lax.ppermute(value, "op", [(0, 1), (1, 0)])


def plan(nvec, sectors, early):
    inner = [*range(QMAX, sectors - QMAX)]
    edge = [*range(QMAX), *range(sectors - QMAX, sectors)]
    first, rest = inner[:early], inner[early:] + edge
    return [[(v, t) for t in ts for v in range(nvec)] for ts in (first, rest)]


class Work:
    def __init__(self, refs, psi, left, right, shifts, active, me):
        self.ext, self.lbuf, self.rbuf, self.obuf, self.sem_p, self.sem_l, self.sem_r, self.sem_o = refs
        self.psi, self.left, self.right, self.shifts, self.active, self.me = psi, left, right, shifts, active, me
        self.nvec = psi.shape[0]

    def operators(self, t):
        one = pl.ds(t, 1)
        return [
            pltpu.make_async_copy(self.left.at[:, one], self.lbuf.at[:, one], self.sem_l.at[t]),
            pltpu.make_async_copy(self.right.at[:, one], self.rbuf.at[:, one], self.sem_r.at[t]),
        ]

    def source(self, s):
        return pltpu.make_async_copy(self.psi.at[:, pl.ds(s, 1)], self.ext.at[:, pl.ds(s + QMAX, 1)], self.sem_p.at[s])

    def stores(self, job, mine, theirs):
        return [
            pltpu.make_async_copy(self.obuf.at[self.me, job], mine.at[job], self.sem_o.at[0, job]),
            pltpu.make_async_copy(self.obuf.at[1 - self.me, job], theirs.at[job], self.sem_o.at[1, job]),
        ]

    def product(self, v, t, job):
        count, _, _, blk = self.left.shape
        half = blk // 2
        middles = []
        for k in range(count):
            source = self.ext[v, t + QMAX - self.shifts[k]]
            middle = jnp.dot(self.lbuf[k, t], source, preferred_element_type=F32)
            middles.append((middle * self.active[k, t].astype(F32)).astype(B16))
        rights = jnp.concatenate([self.rbuf[k, t] for k in range(count)], axis=1)
        total = lax.dot_general(
            rights, jnp.concatenate(middles, axis=1), (((1,), (1,)), ((), ())), preferred_element_type=F32
        )
        for h in range(2):
            self.obuf[h, job] = total[:, h * half : (h + 1) * half].astype(B16)

    def start(self, first, count):
        for s in range(first - QMAX, first + QMAX):
            self.source(s).start()
        for t in range(first, first + count):
            self.source(t + QMAX).start()
            for copy in self.operators(t):
                copy.start()

    def sector(self, t, base, mine, theirs):
        for copy in self.operators(t):
            copy.wait()
        for v in range(self.nvec):
            self.product(v, t, base + v)
        for v in range(self.nvec):
            for copy in self.stores(base + v, mine, theirs):
                copy.start()

    def inner(self, first, count, mine, theirs):
        for s in range(first - QMAX, first + QMAX):
            self.source(s).wait()

        def body(index, carry):
            self.source(first + index + QMAX).wait()
            self.sector(first + index, index * self.nvec, mine, theirs)
            return carry

        lax.fori_loop(0, count, body, 0)

    def finish(self, jobs, mine, theirs):
        def body(job, carry):
            for copy in self.stores(job, mine, theirs):
                copy.wait()
            return carry

        lax.fori_loop(0, jobs, body, 0)


def first_kernel(early, me_ref, shifts, active, psi, left, right, mine, theirs, *refs):
    work = Work(refs, psi, left, right, shifts, active, me_ref[0])
    work.start(QMAX, early)
    work.inner(QMAX, early, mine, theirs)
    work.finish(mine.shape[0], mine, theirs)


def second_kernel(early, me_ref, shifts, active, psi, left, right, halo, other, mine, theirs, *refs):
    nvec, sectors = psi.shape[:2]
    me = me_ref[0]
    *refs, sem_h = refs
    work = Work(refs, psi, left, right, shifts, active, me)
    sides = []
    for index, (source, core) in enumerate(((halo, me), (other, 1 - me))):
        at = core * (sectors + QMAX)
        sides.append(pltpu.make_async_copy(source, work.ext.at[:, pl.ds(at, QMAX)], sem_h.at[index]))
    first, count = QMAX + early, sectors - 2 * QMAX - early
    sides += [work.source(s) for s in range(min(2 * QMAX, first - QMAX))]
    work.start(first, count)
    edge = [*range(QMAX), *range(sectors - QMAX, sectors)]
    for copy in sides:
        copy.start()
    for t in edge:
        for copy in work.operators(t):
            copy.start()
    work.inner(first, count, mine, theirs)
    for copy in sides:
        copy.wait()
    for side, at in enumerate((0, sectors + QMAX)):

        @pl.when(me_ref[1 + side] == 1)
        def _(at=at):
            work.ext[:, at : at + QMAX] = jnp.zeros((nvec, QMAX) + psi.shape[2:], psi.dtype)

    for place, t in enumerate(edge):
        work.sector(t, (count + place) * nvec, mine, theirs)
    work.finish(mine.shape[0], mine, theirs)


def products(kernel, early, jobs, me, shifts, active, psi, left, right, *more):
    count, sectors, blk, _ = left.shape
    half = blk // 2
    smem = pl.BlockSpec(memory_space=pltpu.SMEM)
    hbm = pl.BlockSpec(memory_space=pl.ANY)
    out = jax.ShapeDtypeStruct((jobs, blk, half), B16)
    return pl.pallas_call(
        functools.partial(kernel, early),
        out_shape=(out, out),
        in_specs=[smem] * 3 + [hbm] * 3 + [hbm] * len(more),
        out_specs=(hbm, hbm),
        scratch_shapes=[
            pltpu.VMEM((psi.shape[0], sectors + 2 * QMAX, blk, blk), B16),
            pltpu.VMEM((count, sectors, blk, blk), B16),
            pltpu.VMEM((count, sectors, blk, blk), B16),
            pltpu.VMEM((2, jobs, blk, half), B16),
            pltpu.SemaphoreType.DMA((sectors,)),
            pltpu.SemaphoreType.DMA((sectors,)),
            pltpu.SemaphoreType.DMA((sectors,)),
            pltpu.SemaphoreType.DMA((2, jobs)),
        ]
        + ([pltpu.SemaphoreType.DMA((2,))] if more else []),
        compiler_params=pltpu.CompilerParams(vmem_limit_bytes=60 * 2**20),
        cost_estimate=pl.CostEstimate(flops=2 * jobs * 2 * count * blk**3, bytes_accessed=12 * 2**20, transcendentals=0),
        name=kernel.__name__,
    )(me, shifts, active, psi, left, right, *more)


def combine_kernel(parts, behind, *refs):
    pairs, refs = refs[: 2 * parts], refs[2 * parts + behind :]
    owned, (obuf, sem) = refs[0], refs[-2:]
    size, _, share, half = obuf.shape
    base = 0
    for part in range(parts):
        abuf, bbuf = pairs[2 * part], pairs[2 * part + 1]
        for job in range(abuf.shape[0]):
            total = (abuf[job].astype(F32) + bbuf[job].astype(F32)).astype(B16)
            obuf[:, base + job] = total.reshape(size, share, half)
        base += abuf.shape[0]
    store = pltpu.make_async_copy(obuf, owned, sem.at[0])
    store.start()
    store.wait()


def combine(pairs, size, *behind):
    refs = [ref for pair in pairs for ref in pair]
    jobs = sum(mine.shape[0] for mine, _ in pairs)
    _, blk, half = refs[0].shape
    hbm = pl.BlockSpec(memory_space=pl.ANY)
    block = (size, jobs, blk // size, half)
    return pl.pallas_call(
        functools.partial(combine_kernel, len(pairs), len(behind)),
        out_shape=jax.ShapeDtypeStruct(block, B16),
        in_specs=[pl.BlockSpec(memory_space=pltpu.VMEM)] * len(refs) + [hbm] * len(behind),
        out_specs=hbm,
        scratch_shapes=[pltpu.VMEM(block, B16), pltpu.SemaphoreType.DMA((1,))],
        compiler_params=pltpu.CompilerParams(vmem_limit_bytes=16 * 2**20),
        cost_estimate=pl.CostEstimate(flops=0, bytes_accessed=0, transcendentals=0),
        name="combine",
    )(*refs, *behind)


def arrange_kernel(plans, sectors, *refs):
    count = len(plans)
    views, out, bufs, (acc, obuf, sem) = refs[:count], refs[count], refs[count + 1 : 2 * count + 1], refs[2 * count + 1 :]
    size, _, share, _ = bufs[0].shape
    loads = [pltpu.make_async_copy(view, buf, sem.at[index]) for index, (view, buf) in enumerate(zip(views, bufs))]
    for copy in loads:
        copy.start()
    for copy in loads:
        copy.wait()

    def body(source, carry):
        for buf, jobs in zip(bufs, plans):
            for job, (v, t) in enumerate(jobs):
                acc[v, pl.ds(source * sectors + t, share, stride=size * sectors), :] = buf[source, job].astype(F32)
        return carry

    lax.fori_loop(0, size, body, 0)
    stores = []
    for v in range(obuf.shape[0]):
        obuf[v] = acc[v].astype(B16)
        stores.append(pltpu.make_async_copy(obuf.at[v], out.at[v], sem.at[count + v]))
        stores[-1].start()
    for copy in stores:
        copy.wait()


def arrange(plans, views, nvec, sectors):
    size, _, share, half = views[0].shape
    rows = share * size * sectors
    hbm = pl.BlockSpec(memory_space=pl.ANY)
    out = pl.pallas_call(
        functools.partial(arrange_kernel, plans, sectors),
        out_shape=jax.ShapeDtypeStruct((nvec, rows, half), B16),
        in_specs=[hbm] * len(views),
        out_specs=hbm,
        scratch_shapes=[pltpu.VMEM(view.shape, B16) for view in views]
        + [
            pltpu.VMEM((nvec, rows, half), F32),
            pltpu.VMEM((nvec, rows, half), B16),
            pltpu.SemaphoreType.DMA((len(views) + nvec,)),
        ],
        compiler_params=pltpu.CompilerParams(vmem_limit_bytes=24 * 2**20),
        name="arrange",
    )(*views)
    return out.reshape(nvec, share, size * sectors, half)


def general(psi, left_ops, right_ops, shifts, active):
    before, after = neighbours(psi, QMAX)
    padded = jnp.concatenate([before, psi, after], axis=1)
    count = left_ops.shape[0]
    nvec, sectors, blk, _ = psi.shape

    def add_term(index, total):
        source = lax.dynamic_slice_in_dim(padded, QMAX - shifts[index], sectors, 1)
        middle = jnp.einsum("tij,vtjk->vtik", left_ops[index], source, preferred_element_type=F32).astype(B16)
        term = jnp.einsum("vtik,tlk->vlti", middle, right_ops[index], preferred_element_type=F32)
        weight = active[index].astype(F32)
        return total + term * weight[None, None, :, None]

    total = lax.fori_loop(0, count, add_term, jnp.zeros((nvec, blk, sectors, blk), F32))
    summed = lax.psum(total, "op")
    share = blk // lax.axis_size("op")
    owned = lax.dynamic_slice_in_dim(summed, lax.axis_index("op") * share, share, 3)
    return lax.all_to_all(owned.astype(B16), "sec", split_axis=1, concat_axis=2, tiled=True)


def per_device(psi, left_ops, right_ops, shifts, active):
    nvec, sectors, blk, _ = psi.shape
    size, half = lax.axis_size("sec"), blk // 2
    if lax.axis_size("op") != 2 or sectors <= 2 * QMAX or blk % (16 * size):
        return general(psi, left_ops, right_ops, shifts, active)
    me = lax.axis_index("op")
    sec = lax.axis_index("sec")
    place = jnp.stack([me, (sec == 0).astype(jnp.int32), (sec == size - 1).astype(jnp.int32)])
    state = (place, shifts, active, psi, left_ops, right_ops)
    early = 4
    first, rest = plan(nvec, sectors, early)

    def fence(make, jobs, *operands):
        zeros = lambda *_: (jnp.zeros((len(jobs), blk, half), B16),) * 2
        return lax.cond(sec < size, make, zeros, *operands)

    def begin(*state):
        mine, theirs = products(first_kernel, early, len(first), *state)
        return mine, swap(theirs)

    def go_on(*state):
        mine, theirs = products(second_kernel, early, len(rest), *state)
        return mine, swap(theirs)

    halo = fetch(psi, me)
    owned = combine([fence(begin, first, *state)], size, halo)
    views = [lax.all_to_all(owned, "sec", split_axis=0, concat_axis=0, tiled=True)]
    pair = fence(go_on, rest, *state, halo, swap(halo))
    owned = combine([pair], size)
    views.append(lax.all_to_all(owned, "sec", split_axis=0, concat_axis=0, tiled=True))
    return arrange([first, rest], views, nvec, sectors)


def solution(mesh):
    placed = (
        P(None, "sec", None, None),
        P("op", "sec", None, None),
        P("op", "sec", None, None),
        P("op"),
        P("op", "sec"),
    )
    return jax.shard_map(
        per_device,
        mesh=mesh,
        in_specs=placed,
        out_specs=P(None, "sec", None, "op"),
        check_vma=False,
    )
```

```python
import functools

import jax
import jax.numpy as jnp
from jax import lax
from jax.experimental import pallas as pl
from jax.experimental.pallas import tpu as pltpu
from jax.sharding import PartitionSpec as P

QMAX = 1
F32, B16 = jnp.float32, jnp.bfloat16


def neighbours(value, width):
    size, length = lax.axis_size("sec"), value.shape[1]
    up = [(i, i + 1) for i in range(size - 1)]
    down = [(j, i) for i, j in up]
    before = lax.ppermute(lax.slice_in_dim(value, length - width, length, axis=1), "sec", up)
    after = lax.ppermute(lax.slice_in_dim(value, 0, width, axis=1), "sec", down)
    return before, after


def fetch(psi, me):
    size, sectors = lax.axis_size("sec"), psi.shape[1]
    ahead = [(i, i + 1) for i in range(size - 1)]
    back = [(size + j, size + i) for i, j in ahead]
    turns = [(size - 1, 2 * size - 1), (size, 0)]
    part = lax.dynamic_slice_in_dim(psi, (1 - me) * (sectors - QMAX), QMAX, axis=1)
    return lax.ppermute(part, ("op", "sec"), ahead + turns + back)


def swap(value):
    return lax.ppermute(value, "op", [(0, 1), (1, 0)])


def plan(nvec, sectors, early):
    inner = [*range(QMAX, sectors - QMAX)]
    edge = [*range(QMAX), *range(sectors - QMAX, sectors)]
    first, rest = inner[:early], inner[early:] + edge
    return [[(v, t) for t in ts for v in range(nvec)] for ts in (first, rest)]


class Work:
    def __init__(self, refs, psi, left, right, shifts, active, me):
        self.ext, self.lbuf, self.rbuf, self.sem_p, self.sem_l, self.sem_r = refs
        self.psi, self.left, self.right, self.shifts, self.active, self.me = psi, left, right, shifts, active, me
        self.nvec = psi.shape[0]

    def operators(self, t):
        one = pl.ds(t, 1)
        return [
            pltpu.make_async_copy(self.left.at[:, one], self.lbuf.at[:, one], self.sem_l.at[t]),
            pltpu.make_async_copy(self.right.at[:, one], self.rbuf.at[:, one], self.sem_r.at[t]),
        ]

    def source(self, s):
        return pltpu.make_async_copy(self.psi.at[:, pl.ds(s, 1)], self.ext.at[:, pl.ds(s + QMAX, 1)], self.sem_p.at[s])

    def products(self, t, base, mine, theirs):
        count, _, _, blk = self.left.shape
        half = blk // 2
        middles = []
        for k in range(count):
            sources = jnp.concatenate([self.ext[v, t + QMAX - self.shifts[k]] for v in range(self.nvec)], axis=1)
            middle = jnp.dot(self.lbuf[k, t], sources, preferred_element_type=F32)
            middles.append((middle * self.active[k, t].astype(F32)).astype(B16))
        rights = jnp.concatenate([self.rbuf[k, t] for k in range(count)], axis=1)
        for v in range(self.nvec):
            middle = jnp.concatenate([m[:, v * blk : (v + 1) * blk] for m in middles], axis=1)
            total = lax.dot_general(rights, middle, (((1,), (1,)), ((), ())), preferred_element_type=F32)
            low, high = total[:, :half], total[:, half:]
            mine[base + v] = jnp.where(self.me == 0, low, high).astype(B16)
            theirs[base + v] = jnp.where(self.me == 0, high, low).astype(B16)

    def start(self, first, count):
        for s in range(first - QMAX, first + QMAX):
            self.source(s).start()
        for t in range(first, first + count):
            self.source(t + QMAX).start()
            for copy in self.operators(t):
                copy.start()

    def sector(self, t, base, mine, theirs):
        for copy in self.operators(t):
            copy.wait()
        self.products(t, base, mine, theirs)

    def inner(self, first, count, mine, theirs):
        for s in range(first - QMAX, first + QMAX):
            self.source(s).wait()

        def body(index, carry):
            self.source(first + index + QMAX).wait()
            self.sector(first + index, index * self.nvec, mine, theirs)
            return carry

        lax.fori_loop(0, count, body, 0)


def first_kernel(early, me_ref, shifts, active, psi, left, right, mine, theirs, *refs):
    work = Work(refs, psi, left, right, shifts, active, me_ref[0])
    work.start(QMAX, early)
    work.inner(QMAX, early, mine, theirs)


def second_kernel(early, me_ref, shifts, active, psi, left, right, halo, other, mine, theirs, *refs):
    nvec, sectors = psi.shape[:2]
    me = me_ref[0]
    *refs, sem_h = refs
    work = Work(refs, psi, left, right, shifts, active, me)
    sides = []
    for index, (source, core) in enumerate(((halo, me), (other, 1 - me))):
        at = core * (sectors + QMAX)
        sides.append(pltpu.make_async_copy(source, work.ext.at[:, pl.ds(at, QMAX)], sem_h.at[index]))
    first, count = QMAX + early, sectors - 2 * QMAX - early
    sides += [work.source(s) for s in range(min(2 * QMAX, first - QMAX))]
    work.start(first, count)
    edge = [*range(QMAX), *range(sectors - QMAX, sectors)]
    for copy in sides:
        copy.start()
    for t in edge:
        for copy in work.operators(t):
            copy.start()
    work.inner(first, count, mine, theirs)
    for copy in sides:
        copy.wait()
    for side, at in enumerate((0, sectors + QMAX)):

        @pl.when(me_ref[1 + side] == 1)
        def _(at=at):
            work.ext[:, at : at + QMAX] = jnp.zeros((nvec, QMAX) + psi.shape[2:], psi.dtype)

    for place, t in enumerate(edge):
        work.sector(t, (count + place) * nvec, mine, theirs)


def products(kernel, early, jobs, me, shifts, active, psi, left, right, *more):
    count, sectors, blk, _ = left.shape
    half = blk // 2
    smem = pl.BlockSpec(memory_space=pltpu.SMEM)
    hbm = pl.BlockSpec(memory_space=pl.ANY)
    out = jax.ShapeDtypeStruct((jobs, blk, half), B16)
    return pl.pallas_call(
        functools.partial(kernel, early),
        out_shape=(out, out),
        in_specs=[smem] * 3 + [hbm] * 3 + [hbm] * len(more),
        out_specs=(pl.BlockSpec(memory_space=pltpu.VMEM),) * 2,
        scratch_shapes=[
            pltpu.VMEM((psi.shape[0], sectors + 2 * QMAX, blk, blk), B16),
            pltpu.VMEM((count, sectors, blk, blk), B16),
            pltpu.VMEM((count, sectors, blk, blk), B16),
            pltpu.SemaphoreType.DMA((sectors,)),
            pltpu.SemaphoreType.DMA((sectors,)),
            pltpu.SemaphoreType.DMA((sectors,)),
        ]
        + ([pltpu.SemaphoreType.DMA((2,))] if more else []),
        compiler_params=pltpu.CompilerParams(vmem_limit_bytes=40 * 2**20),
        cost_estimate=pl.CostEstimate(flops=2 * jobs * 2 * count * blk**3, bytes_accessed=12 * 2**20, transcendentals=0),
        name=kernel.__name__,
    )(me, shifts, active, psi, left, right, *more)


def combine_kernel(parts, behind, *refs):
    pairs, refs = refs[: 2 * parts], refs[2 * parts + behind :]
    owned, (obuf, sem) = refs[0], refs[-2:]
    size, _, share, half = obuf.shape
    base = 0
    for part in range(parts):
        abuf, bbuf = pairs[2 * part], pairs[2 * part + 1]
        for job in range(abuf.shape[0]):
            total = (abuf[job].astype(F32) + bbuf[job].astype(F32)).astype(B16)
            obuf[:, base + job] = total.reshape(size, share, half)
        base += abuf.shape[0]
    store = pltpu.make_async_copy(obuf, owned, sem.at[0])
    store.start()
    store.wait()


def after_kernel(value, earlier, out):
    pass


def after(value, earlier):
    hbm = pl.BlockSpec(memory_space=pl.ANY)
    return pl.pallas_call(
        after_kernel,
        out_shape=jax.ShapeDtypeStruct(value.shape, value.dtype),
        in_specs=[hbm, hbm],
        out_specs=hbm,
        input_output_aliases={0: 0},
        name="after",
    )(value, earlier)


def combine(pairs, size, *behind):
    refs = [ref for pair in pairs for ref in pair]
    jobs = sum(mine.shape[0] for mine, _ in pairs)
    _, blk, half = refs[0].shape
    hbm = pl.BlockSpec(memory_space=pl.ANY)
    block = (size, jobs, blk // size, half)
    return pl.pallas_call(
        functools.partial(combine_kernel, len(pairs), len(behind)),
        out_shape=jax.ShapeDtypeStruct(block, B16),
        in_specs=[pl.BlockSpec(memory_space=pltpu.VMEM)] * len(refs) + [hbm] * len(behind),
        out_specs=hbm,
        scratch_shapes=[pltpu.VMEM(block, B16), pltpu.SemaphoreType.DMA((1,))],
        compiler_params=pltpu.CompilerParams(vmem_limit_bytes=16 * 2**20),
        cost_estimate=pl.CostEstimate(flops=0, bytes_accessed=0, transcendentals=0),
        name="combine",
    )(*refs, *behind)


def arrange_kernel(plans, sectors, *refs):
    count = len(plans)
    views, out, (acc, obuf, sem) = refs[:count], refs[count], refs[count + 1 :]
    size, _, share, _ = views[0].shape
    stores = []
    for vector in range(obuf.shape[0]):

        def body(source, carry, vector=vector):
            for view, jobs in zip(views, plans):
                for job, (v, t) in enumerate(jobs):
                    if v == vector:
                        rows = pl.ds(source * sectors + t, share, stride=size * sectors)
                        acc[vector, rows, :] = view[source, job].astype(F32)
            return carry

        lax.fori_loop(0, size, body, 0, unroll=2)
        obuf[vector] = acc[vector].astype(B16)
        stores.append(pltpu.make_async_copy(obuf.at[vector], out.at[vector], sem.at[vector]))
        stores[-1].start()
    for copy in stores:
        copy.wait()


def arrange(plans, views, nvec, sectors):
    size, _, share, half = views[0].shape
    rows = share * size * sectors
    out = pl.pallas_call(
        functools.partial(arrange_kernel, plans, sectors),
        out_shape=jax.ShapeDtypeStruct((nvec, rows, half), B16),
        in_specs=[pl.BlockSpec(memory_space=pltpu.VMEM)] * len(views),
        out_specs=pl.BlockSpec(memory_space=pl.ANY),
        scratch_shapes=[
            pltpu.VMEM((nvec, rows, half), F32),
            pltpu.VMEM((nvec, rows, half), B16),
            pltpu.SemaphoreType.DMA((nvec,)),
        ],
        compiler_params=pltpu.CompilerParams(vmem_limit_bytes=24 * 2**20),
        name="arrange",
    )(*views)
    return out.reshape(nvec, share, size * sectors, half)


def general(psi, left_ops, right_ops, shifts, active):
    before, after = neighbours(psi, QMAX)
    padded = jnp.concatenate([before, psi, after], axis=1)
    count = left_ops.shape[0]
    nvec, sectors, blk, _ = psi.shape

    def add_term(index, total):
        source = lax.dynamic_slice_in_dim(padded, QMAX - shifts[index], sectors, 1)
        middle = jnp.einsum("tij,vtjk->vtik", left_ops[index], source, preferred_element_type=F32).astype(B16)
        term = jnp.einsum("vtik,tlk->vlti", middle, right_ops[index], preferred_element_type=F32)
        weight = active[index].astype(F32)
        return total + term * weight[None, None, :, None]

    total = lax.fori_loop(0, count, add_term, jnp.zeros((nvec, blk, sectors, blk), F32))
    summed = lax.psum(total, "op")
    share = blk // lax.axis_size("op")
    owned = lax.dynamic_slice_in_dim(summed, lax.axis_index("op") * share, share, 3)
    return lax.all_to_all(owned.astype(B16), "sec", split_axis=1, concat_axis=2, tiled=True)


def per_device(psi, left_ops, right_ops, shifts, active):
    nvec, sectors, blk, _ = psi.shape
    size, half = lax.axis_size("sec"), blk // 2
    if lax.axis_size("op") != 2 or sectors <= 2 * QMAX or blk % (16 * size):
        return general(psi, left_ops, right_ops, shifts, active)
    me = lax.axis_index("op")
    sec = lax.axis_index("sec")
    place = jnp.stack([me, (sec == 0).astype(jnp.int32), (sec == size - 1).astype(jnp.int32)])
    state = (place, shifts, active, psi, left_ops, right_ops)
    early = 3
    first, rest = plan(nvec, sectors, early)

    def fence(kernel, jobs, *operands):
        def make(*operands):
            mine, theirs = products(kernel, early, len(jobs), *operands)
            return combine([(mine, swap(theirs))], size)

        zeros = lambda *_: jnp.zeros((size, len(jobs), blk // size, half), B16)
        return lax.cond(sec < size, make, zeros, *operands)

    halo = fetch(psi, me)
    owned = after(fence(first_kernel, first, *state), halo)
    views = [lax.all_to_all(owned, "sec", split_axis=0, concat_axis=0, tiled=True)]
    owned = fence(second_kernel, rest, *state, halo, swap(halo))
    views.append(lax.all_to_all(owned, "sec", split_axis=0, concat_axis=0, tiled=True))
    return arrange([first, rest], views, nvec, sectors)


def solution(mesh):
    placed = (
        P(None, "sec", None, None),
        P("op", "sec", None, None),
        P("op", "sec", None, None),
        P("op"),
        P("op", "sec"),
    )
    return jax.shard_map(
        per_device,
        mesh=mesh,
        in_specs=placed,
        out_specs=P(None, "sec", None, "op"),
        check_vma=False,
    )
```

```python
import functools

import jax
import jax.numpy as jnp
from jax import lax
from jax.experimental import pallas as pl
from jax.experimental.pallas import tpu as pltpu
from jax.sharding import PartitionSpec as P

QMAX = 1
F32, B16 = jnp.float32, jnp.bfloat16


def neighbours(value, width):
    size, length = lax.axis_size("sec"), value.shape[1]
    up = [(i, i + 1) for i in range(size - 1)]
    down = [(j, i) for i, j in up]
    before = lax.ppermute(lax.slice_in_dim(value, length - width, length, axis=1), "sec", up)
    after = lax.ppermute(lax.slice_in_dim(value, 0, width, axis=1), "sec", down)
    return before, after


def fetch(psi, me):
    size, sectors = lax.axis_size("sec"), psi.shape[1]
    ahead = [(i, i + 1) for i in range(size - 1)]
    back = [(size + j, size + i) for i, j in ahead]
    turns = [(size - 1, 2 * size - 1), (size, 0)]
    part = lax.dynamic_slice_in_dim(psi, (1 - me) * (sectors - QMAX), QMAX, axis=1)
    return lax.ppermute(part, ("op", "sec"), ahead + turns + back)


def swap(value):
    return lax.ppermute(value, "op", [(0, 1), (1, 0)])


def plan(nvec, sectors, early):
    inner = [*range(QMAX, sectors - QMAX)]
    edge = [*range(QMAX), *range(sectors - QMAX, sectors)]
    first, rest = inner[:early], inner[early:] + edge
    return [[(v, t) for t in ts for v in range(nvec)] for ts in (first, rest)]


class Work:
    def __init__(self, refs, psi, left, right, shifts, active, me):
        self.ext, self.lbuf, self.rbuf, self.sem_p, self.sem_l, self.sem_r = refs
        self.psi, self.left, self.right, self.shifts, self.active, self.me = psi, left, right, shifts, active, me
        self.nvec = psi.shape[0]

    def operators(self, t):
        one = pl.ds(t, 1)
        return [
            pltpu.make_async_copy(self.left.at[:, one], self.lbuf.at[:, one], self.sem_l.at[t]),
            pltpu.make_async_copy(self.right.at[:, one], self.rbuf.at[:, one], self.sem_r.at[t]),
        ]

    def source(self, s):
        return pltpu.make_async_copy(self.psi.at[:, pl.ds(s, 1)], self.ext.at[:, pl.ds(s + QMAX, 1)], self.sem_p.at[s])

    def products(self, t, base, mine, theirs):
        count, _, _, blk = self.left.shape
        half = blk // 2
        middles = []
        for k in range(count):
            sources = jnp.concatenate([self.ext[v, t + QMAX - self.shifts[k]] for v in range(self.nvec)], axis=1)
            middle = jnp.dot(self.lbuf[k, t], sources, preferred_element_type=F32)
            middles.append((middle * self.active[k, t].astype(F32)).astype(B16))
        rights = jnp.concatenate([self.rbuf[k, t] for k in range(count)], axis=1)
        for v in range(self.nvec):
            middle = jnp.concatenate([m[:, v * blk : (v + 1) * blk] for m in middles], axis=1)
            total = lax.dot_general(rights, middle, (((1,), (1,)), ((), ())), preferred_element_type=F32)
            low, high = total[:, :half], total[:, half:]
            mine[base + v] = jnp.where(self.me == 0, low, high).astype(B16)
            theirs[base + v] = jnp.where(self.me == 0, high, low).astype(B16)

    def start(self, first, count):
        for s in range(first - QMAX, first + QMAX):
            self.source(s).start()
        for t in range(first, first + count):
            self.source(t + QMAX).start()
            for copy in self.operators(t):
                copy.start()

    def sector(self, t, base, mine, theirs):
        for copy in self.operators(t):
            copy.wait()
        self.products(t, base, mine, theirs)

    def inner(self, first, count, mine, theirs):
        for s in range(first - QMAX, first + QMAX):
            self.source(s).wait()

        def body(index, carry):
            self.source(first + index + QMAX).wait()
            self.sector(first + index, index * self.nvec, mine, theirs)
            return carry

        lax.fori_loop(0, count, body, 0)


def first_kernel(early, me_ref, shifts, active, psi, left, right, mine, theirs, *refs):
    work = Work(refs, psi, left, right, shifts, active, me_ref[0])
    work.start(QMAX, early)
    work.inner(QMAX, early, mine, theirs)


def second_kernel(early, me_ref, shifts, active, psi, left, right, halo, other, mine, theirs, *refs):
    nvec, sectors = psi.shape[:2]
    me = me_ref[0]
    *refs, sem_h = refs
    work = Work(refs, psi, left, right, shifts, active, me)
    sides = []
    for index, (source, core) in enumerate(((halo, me), (other, 1 - me))):
        at = core * (sectors + QMAX)
        sides.append(pltpu.make_async_copy(source, work.ext.at[:, pl.ds(at, QMAX)], sem_h.at[index]))
    first, count = QMAX + early, sectors - 2 * QMAX - early
    sides += [work.source(s) for s in range(min(2 * QMAX, first - QMAX))]
    work.start(first, count)
    edge = [*range(QMAX), *range(sectors - QMAX, sectors)]
    for copy in sides:
        copy.start()
    for t in edge:
        for copy in work.operators(t):
            copy.start()
    work.inner(first, count, mine, theirs)
    for copy in sides:
        copy.wait()
    for side, at in enumerate((0, sectors + QMAX)):

        @pl.when(me_ref[1 + side] == 1)
        def _(at=at):
            work.ext[:, at : at + QMAX] = jnp.zeros((nvec, QMAX) + psi.shape[2:], psi.dtype)

    for place, t in enumerate(edge):
        work.sector(t, (count + place) * nvec, mine, theirs)


def products(kernel, early, jobs, me, shifts, active, psi, left, right, *more):
    count, sectors, blk, _ = left.shape
    half = blk // 2
    smem = pl.BlockSpec(memory_space=pltpu.SMEM)
    hbm = pl.BlockSpec(memory_space=pl.ANY)
    out = jax.ShapeDtypeStruct((jobs, blk, half), B16)
    return pl.pallas_call(
        functools.partial(kernel, early),
        out_shape=(out, out),
        in_specs=[smem] * 3 + [hbm] * 3 + [hbm] * len(more),
        out_specs=(pl.BlockSpec(memory_space=pltpu.VMEM),) * 2,
        scratch_shapes=[
            pltpu.VMEM((psi.shape[0], sectors + 2 * QMAX, blk, blk), B16),
            pltpu.VMEM((count, sectors, blk, blk), B16),
            pltpu.VMEM((count, sectors, blk, blk), B16),
            pltpu.SemaphoreType.DMA((sectors,)),
            pltpu.SemaphoreType.DMA((sectors,)),
            pltpu.SemaphoreType.DMA((sectors,)),
        ]
        + ([pltpu.SemaphoreType.DMA((2,))] if more else []),
        compiler_params=pltpu.CompilerParams(vmem_limit_bytes=40 * 2**20),
        cost_estimate=pl.CostEstimate(flops=2 * jobs * 2 * count * blk**3, bytes_accessed=12 * 2**20, transcendentals=0),
        name=kernel.__name__,
    )(me, shifts, active, psi, left, right, *more)


def combine_kernel(parts, behind, *refs):
    pairs, refs = refs[: 2 * parts], refs[2 * parts + behind :]
    owned, (obuf, sem) = refs[0], refs[-2:]
    size, _, share, half = obuf.shape
    base = 0
    for part in range(parts):
        abuf, bbuf = pairs[2 * part], pairs[2 * part + 1]
        for job in range(abuf.shape[0]):
            total = (abuf[job].astype(F32) + bbuf[job].astype(F32)).astype(B16)
            obuf[:, base + job] = total.reshape(size, share, half)
        base += abuf.shape[0]
    store = pltpu.make_async_copy(obuf, owned, sem.at[0])
    store.start()
    store.wait()


def after_kernel(value, earlier, out):
    pass


def after(value, earlier):
    hbm = pl.BlockSpec(memory_space=pl.ANY)
    return pl.pallas_call(
        after_kernel,
        out_shape=jax.ShapeDtypeStruct(value.shape, value.dtype),
        in_specs=[hbm, hbm],
        out_specs=hbm,
        input_output_aliases={0: 0},
        name="after",
    )(value, earlier)


def combine(pairs, size, *behind):
    refs = [ref for pair in pairs for ref in pair]
    jobs = sum(mine.shape[0] for mine, _ in pairs)
    _, blk, half = refs[0].shape
    hbm = pl.BlockSpec(memory_space=pl.ANY)
    block = (size, jobs, blk // size, half)
    return pl.pallas_call(
        functools.partial(combine_kernel, len(pairs), len(behind)),
        out_shape=jax.ShapeDtypeStruct(block, B16),
        in_specs=[pl.BlockSpec(memory_space=pltpu.VMEM)] * len(refs) + [hbm] * len(behind),
        out_specs=hbm,
        scratch_shapes=[pltpu.VMEM(block, B16), pltpu.SemaphoreType.DMA((1,))],
        compiler_params=pltpu.CompilerParams(vmem_limit_bytes=16 * 2**20),
        cost_estimate=pl.CostEstimate(flops=0, bytes_accessed=0, transcendentals=0),
        name="combine",
    )(*refs, *behind)


def arrange_kernel(plans, sectors, *refs):
    count = len(plans)
    views, out, (acc, obuf, sem) = refs[:count], refs[count], refs[count + 1 :]
    size, _, share, _ = views[0].shape
    stores = []
    for vector in range(obuf.shape[0]):

        def body(source, carry, vector=vector):
            base = source * share * sectors
            for view, jobs in zip(views, plans):
                for job, (v, t) in enumerate(jobs):
                    if v == vector:
                        acc[vector, pl.ds(base + t, share, stride=sectors), :] = view[source, job].astype(F32)
            return carry

        lax.fori_loop(0, size, body, 0, unroll=2)
        tiles = acc[vector].reshape(size, share, sectors, acc.shape[2])
        obuf[vector] = jnp.swapaxes(tiles, 0, 1).reshape(obuf.shape[1:]).astype(B16)
        stores.append(pltpu.make_async_copy(obuf.at[vector], out.at[vector], sem.at[vector]))
        stores[-1].start()
    for copy in stores:
        copy.wait()


def arrange(plans, views, nvec, sectors):
    size, _, share, half = views[0].shape
    rows = share * size * sectors
    out = pl.pallas_call(
        functools.partial(arrange_kernel, plans, sectors),
        out_shape=jax.ShapeDtypeStruct((nvec, rows, half), B16),
        in_specs=[pl.BlockSpec(memory_space=pltpu.VMEM)] * len(views),
        out_specs=pl.BlockSpec(memory_space=pl.ANY),
        scratch_shapes=[
            pltpu.VMEM((nvec, rows, half), F32),
            pltpu.VMEM((nvec, rows, half), B16),
            pltpu.SemaphoreType.DMA((nvec,)),
        ],
        compiler_params=pltpu.CompilerParams(vmem_limit_bytes=24 * 2**20),
        name="arrange",
    )(*views)
    return out.reshape(nvec, share, size * sectors, half)


def general(psi, left_ops, right_ops, shifts, active):
    before, after = neighbours(psi, QMAX)
    padded = jnp.concatenate([before, psi, after], axis=1)
    count = left_ops.shape[0]
    nvec, sectors, blk, _ = psi.shape

    def add_term(index, total):
        source = lax.dynamic_slice_in_dim(padded, QMAX - shifts[index], sectors, 1)
        middle = jnp.einsum("tij,vtjk->vtik", left_ops[index], source, preferred_element_type=F32).astype(B16)
        term = jnp.einsum("vtik,tlk->vlti", middle, right_ops[index], preferred_element_type=F32)
        weight = active[index].astype(F32)
        return total + term * weight[None, None, :, None]

    total = lax.fori_loop(0, count, add_term, jnp.zeros((nvec, blk, sectors, blk), F32))
    summed = lax.psum(total, "op")
    share = blk // lax.axis_size("op")
    owned = lax.dynamic_slice_in_dim(summed, lax.axis_index("op") * share, share, 3)
    return lax.all_to_all(owned.astype(B16), "sec", split_axis=1, concat_axis=2, tiled=True)


def per_device(psi, left_ops, right_ops, shifts, active):
    nvec, sectors, blk, _ = psi.shape
    size, half = lax.axis_size("sec"), blk // 2
    if lax.axis_size("op") != 2 or sectors != 8 or blk % (16 * size):
        return general(psi, left_ops, right_ops, shifts, active)
    me = lax.axis_index("op")
    sec = lax.axis_index("sec")
    place = jnp.stack([me, (sec == 0).astype(jnp.int32), (sec == size - 1).astype(jnp.int32)])
    state = (place, shifts, active, psi, left_ops, right_ops)
    early = 3
    first, rest = plan(nvec, sectors, early)

    def fence(kernel, jobs, *operands):
        def make(*operands):
            mine, theirs = products(kernel, early, len(jobs), *operands)
            return combine([(mine, swap(theirs))], size)

        zeros = lambda *_: jnp.zeros((size, len(jobs), blk // size, half), B16)
        return lax.cond(sec < size, make, zeros, *operands)

    halo = fetch(psi, me)
    owned = after(fence(first_kernel, first, *state), halo)
    views = [lax.all_to_all(owned, "sec", split_axis=0, concat_axis=0, tiled=True)]
    owned = fence(second_kernel, rest, *state, halo, swap(halo))
    views.append(lax.all_to_all(owned, "sec", split_axis=0, concat_axis=0, tiled=True))
    return arrange([first, rest], views, nvec, sectors)


def solution(mesh):
    placed = (
        P(None, "sec", None, None),
        P("op", "sec", None, None),
        P("op", "sec", None, None),
        P("op"),
        P("op", "sec"),
    )
    return jax.shard_map(
        per_device,
        mesh=mesh,
        in_specs=placed,
        out_specs=P(None, "sec", None, "op"),
        check_vma=False,
    )
```

```python
import functools

import jax
import jax.numpy as jnp
from jax import lax
from jax.experimental import pallas as pl
from jax.experimental.pallas import tpu as pltpu
from jax.sharding import PartitionSpec as P

QMAX = 1
NEAR = 4
F32, B16 = jnp.float32, jnp.bfloat16


def neighbours(value, width):
    size, length = lax.axis_size("sec"), value.shape[1]
    up = [(i, i + 1) for i in range(size - 1)]
    down = [(j, i) for i, j in up]
    before = lax.ppermute(lax.slice_in_dim(value, length - width, length, axis=1), "sec", up)
    after = lax.ppermute(lax.slice_in_dim(value, 0, width, axis=1), "sec", down)
    return before, after


def fetch(psi, me):
    size, sectors = lax.axis_size("sec"), psi.shape[1]
    ahead = [(i, i + 1) for i in range(size - 1)]
    back = [(size + j, size + i) for i, j in ahead]
    turns = [(size - 1, 2 * size - 1), (size, 0)]
    part = lax.dynamic_slice_in_dim(psi, (1 - me) * (sectors - QMAX), QMAX, axis=1)
    return lax.ppermute(part, ("op", "sec"), ahead + turns + back)


def swap(value):
    return lax.ppermute(value, "op", [(0, 1), (1, 0)])


def plan(nvec, sectors, early):
    inner = [*range(QMAX, sectors - QMAX)]
    edge = [*range(QMAX), *range(sectors - QMAX, sectors)]
    first, rest = inner[:early], inner[early:] + edge
    return [[(v, t) for t in ts for v in range(nvec)] for ts in (first, rest)]


class Work:
    def __init__(self, refs, psi, left, right, shifts, active, me):
        self.ext, self.lbuf, self.rbuf, self.sem_p, self.sem_l, self.sem_r = refs
        self.psi, self.left, self.right, self.shifts, self.active, self.me = psi, left, right, shifts, active, me
        self.nvec = psi.shape[0]

    def operators(self, t):
        one = pl.ds(t, 1)
        return [
            pltpu.make_async_copy(self.left.at[:, one], self.lbuf.at[:, one], self.sem_l.at[t]),
            pltpu.make_async_copy(self.right.at[:, one], self.rbuf.at[:, one], self.sem_r.at[t]),
        ]

    def source(self, s):
        return pltpu.make_async_copy(self.psi.at[:, pl.ds(s, 1)], self.ext.at[:, pl.ds(s + QMAX, 1)], self.sem_p.at[s])

    def products(self, t, base, mine, theirs):
        count, _, _, blk = self.left.shape
        half = blk // 2
        middles = []
        for k in range(count):
            sources = jnp.concatenate([self.ext[v, t + QMAX - self.shifts[k]] for v in range(self.nvec)], axis=1)
            middle = jnp.dot(self.lbuf[k, t], sources, preferred_element_type=F32)
            middles.append((middle * self.active[k, t].astype(F32)).astype(B16))
        rights = jnp.concatenate([self.rbuf[k, t] for k in range(count)], axis=1)
        for v in range(self.nvec):
            middle = jnp.concatenate([m[:, v * blk : (v + 1) * blk] for m in middles], axis=1)
            total = lax.dot_general(rights, middle, (((1,), (1,)), ((), ())), preferred_element_type=F32)
            low, high = total[:, :half], total[:, half:]
            mine[base + v] = jnp.where(self.me == 0, low, high).astype(B16)
            theirs[base + v] = jnp.where(self.me == 0, high, low).astype(B16)

    def start(self, first, count):
        for s in range(first - QMAX, first + QMAX):
            self.source(s).start()
        for t in range(first, first + count):
            self.source(t + QMAX).start()
            for copy in self.operators(t):
                copy.start()

    def sector(self, t, base, mine, theirs):
        for copy in self.operators(t):
            copy.wait()
        self.products(t, base, mine, theirs)

    def inner(self, first, count, mine, theirs):
        for s in range(first - QMAX, first + QMAX):
            self.source(s).wait()

        def body(index, carry):
            self.source(first + index + QMAX).wait()
            self.sector(first + index, index * self.nvec, mine, theirs)
            return carry

        lax.fori_loop(0, count, body, 0)


def first_kernel(early, me_ref, shifts, active, psi, left, right, mine, theirs, *refs):
    work = Work(refs, psi, left, right, shifts, active, me_ref[0])
    work.start(QMAX, early)
    work.inner(QMAX, early, mine, theirs)


def second_kernel(early, me_ref, shifts, active, psi, left, right, halo, other, earlier, mine, theirs, *refs):
    nvec, sectors = psi.shape[:2]
    me = me_ref[0]
    *refs, sem_h = refs
    work = Work(refs, psi, left, right, shifts, active, me)
    sides = []
    for index, (source, core) in enumerate(((halo, me), (other, 1 - me))):
        at = core * (sectors + QMAX)
        sides.append(pltpu.make_async_copy(source, work.ext.at[:, pl.ds(at, QMAX)], sem_h.at[index]))
    first, count = QMAX + early, sectors - 2 * QMAX - early
    sides += [work.source(s) for s in range(min(2 * QMAX, first - QMAX))]
    work.start(first, count)
    edge = [*range(QMAX), *range(sectors - QMAX, sectors)]
    for copy in sides:
        copy.start()
    for t in edge:
        for copy in work.operators(t):
            copy.start()
    work.inner(first, count, mine, theirs)
    for copy in sides:
        copy.wait()
    for side, at in enumerate((0, sectors + QMAX)):

        @pl.when(me_ref[1 + side] == 1)
        def _(at=at):
            work.ext[:, at : at + QMAX] = jnp.zeros((nvec, QMAX) + psi.shape[2:], psi.dtype)

    for place, t in enumerate(edge):
        work.sector(t, (count + place) * nvec, mine, theirs)


def products(kernel, early, jobs, me, shifts, active, psi, left, right, *more):
    count, sectors, blk, _ = left.shape
    half = blk // 2
    smem = pl.BlockSpec(memory_space=pltpu.SMEM)
    hbm = pl.BlockSpec(memory_space=pl.ANY)
    out = jax.ShapeDtypeStruct((jobs, blk, half), B16)
    return pl.pallas_call(
        functools.partial(kernel, early),
        out_shape=(out, out),
        in_specs=[smem] * 3 + [hbm] * 3 + [hbm] * len(more),
        out_specs=(pl.BlockSpec(memory_space=pltpu.VMEM),) * 2,
        scratch_shapes=[
            pltpu.VMEM((psi.shape[0], sectors + 2 * QMAX, blk, blk), B16),
            pltpu.VMEM((count, sectors, blk, blk), B16),
            pltpu.VMEM((count, sectors, blk, blk), B16),
            pltpu.SemaphoreType.DMA((sectors,)),
            pltpu.SemaphoreType.DMA((sectors,)),
            pltpu.SemaphoreType.DMA((sectors,)),
        ]
        + ([pltpu.SemaphoreType.DMA((2,))] if more else []),
        compiler_params=pltpu.CompilerParams(vmem_limit_bytes=40 * 2**20),
        cost_estimate=pl.CostEstimate(flops=2 * jobs * 2 * count * blk**3, bytes_accessed=12 * 2**20, transcendentals=0),
        name=kernel.__name__,
    )(me, shifts, active, psi, left, right, *more)


def combine_kernel(parts, behind, *refs):
    pairs, refs = refs[: 2 * parts], refs[2 * parts + behind :]
    owned, (obuf, sem) = refs[0], refs[-2:]
    size, _, share, half = obuf.shape
    base = 0
    for part in range(parts):
        abuf, bbuf = pairs[2 * part], pairs[2 * part + 1]
        for job in range(abuf.shape[0]):
            total = (abuf[job].astype(F32) + bbuf[job].astype(F32)).astype(B16)
            obuf[:, base + job] = total.reshape(size, share, half)
        base += abuf.shape[0]
    store = pltpu.make_async_copy(obuf, owned, sem.at[0])
    store.start()
    store.wait()


def after_kernel(value, *refs):
    pass


def after(value, *earlier):
    hbm = pl.BlockSpec(memory_space=pl.ANY)
    return pl.pallas_call(
        after_kernel,
        out_shape=jax.ShapeDtypeStruct(value.shape, value.dtype),
        in_specs=[hbm] * (1 + len(earlier)),
        out_specs=hbm,
        input_output_aliases={0: 0},
        name="after",
    )(value, *earlier)


def combine(pairs, size, *behind):
    refs = [ref for pair in pairs for ref in pair]
    jobs = sum(mine.shape[0] for mine, _ in pairs)
    _, blk, half = refs[0].shape
    hbm = pl.BlockSpec(memory_space=pl.ANY)
    block = (size, jobs, blk // size, half)
    return pl.pallas_call(
        functools.partial(combine_kernel, len(pairs), len(behind)),
        out_shape=jax.ShapeDtypeStruct(block, B16),
        in_specs=[pl.BlockSpec(memory_space=pltpu.VMEM)] * len(refs) + [hbm] * len(behind),
        out_specs=hbm,
        scratch_shapes=[pltpu.VMEM(block, B16), pltpu.SemaphoreType.DMA((1,))],
        compiler_params=pltpu.CompilerParams(vmem_limit_bytes=16 * 2**20),
        cost_estimate=pl.CostEstimate(flops=0, bytes_accessed=0, transcendentals=0),
        name="combine",
    )(*refs, *behind)


def blocks_kernel(place, mine, other, *outs):
    rows_of, near = len(outs), outs[0].shape[0]
    share = outs[0].shape[2]
    z, q = place[3], place[4]
    for a, out in enumerate(outs):
        for b in range(near):
            to = lax.rem(z + a, rows_of) * near + lax.rem(q + b, near)
            rows = pl.ds(pl.multiple_of(to * share, share), share)
            out[b] = (mine[:, rows, :].astype(F32) + other[:, rows, :].astype(F32)).astype(B16)


def blocks(place, mine, other, far, near):
    jobs, blk, half = mine.shape
    vmem = pl.BlockSpec(memory_space=pltpu.VMEM)
    block = jax.ShapeDtypeStruct((near, jobs, blk // (far * near), half), B16)
    return pl.pallas_call(
        blocks_kernel,
        out_shape=(block,) * far,
        in_specs=[pl.BlockSpec(memory_space=pltpu.SMEM), vmem, vmem],
        out_specs=(vmem,) * far,
        compiler_params=pltpu.CompilerParams(vmem_limit_bytes=16 * 2**20),
        cost_estimate=pl.CostEstimate(flops=0, bytes_accessed=0, transcendentals=0),
        name="blocks",
    )(place, mine, other)


def regroup_kernel(far, *refs):
    for b, out in enumerate(refs[far:]):
        for a in range(far):
            out[a] = refs[a][b]


def regroup(parts):
    near, *block = parts[0].shape
    vmem = pl.BlockSpec(memory_space=pltpu.VMEM)
    out = jax.ShapeDtypeStruct((len(parts), *block), B16)
    return pl.pallas_call(
        functools.partial(regroup_kernel, len(parts)),
        out_shape=(out,) * near,
        in_specs=[vmem] * len(parts),
        out_specs=(vmem,) * near,
        compiler_params=pltpu.CompilerParams(vmem_limit_bytes=16 * 2**20),
        cost_estimate=pl.CostEstimate(flops=16 * 10**9, bytes_accessed=0, transcendentals=0),
        name="regroup",
    )(*parts)


def arrange_kernel(plans, sectors, place, *refs):
    view, pieces, (out, acc, obuf, sem) = refs[0], refs[1:-4], refs[-4:]
    stepped, direct = plans
    size, _, share, _ = view.shape
    stores = []
    for vector in range(obuf.shape[0]):

        def put(source, job, value, vector=vector):
            v, t = job
            if v == vector:
                acc[vector, pl.ds(source * share * sectors + t, share, stride=sectors), :] = value().astype(F32)

        def body(source, carry):
            for index, job in enumerate(direct):
                put(source, job, lambda: view[source, index])
            return carry

        lax.fori_loop(0, size, body, 0, unroll=2)
        near, far = len(pieces), pieces[0].shape[0]
        for b, piece in enumerate(pieces):
            for a in range(far):
                source = lax.rem(place[3] + far - a, far) * near + lax.rem(place[4] + near - b, near)
                for index, job in enumerate(stepped):
                    put(source, job, lambda: piece[a, index])
        tiles = acc[vector].reshape(size, share, sectors, acc.shape[2])
        obuf[vector] = jnp.swapaxes(tiles, 0, 1).reshape(obuf.shape[1:]).astype(B16)
        stores.append(pltpu.make_async_copy(obuf.at[vector], out.at[vector], sem.at[vector]))
        stores[-1].start()
    for copy in stores:
        copy.wait()


def arrange(plans, sectors, nvec, place, view, pieces):
    size, _, share, half = view.shape
    rows = share * size * sectors
    out = pl.pallas_call(
        functools.partial(arrange_kernel, plans, sectors),
        out_shape=jax.ShapeDtypeStruct((nvec, rows, half), B16),
        in_specs=[pl.BlockSpec(memory_space=pltpu.SMEM)]
        + [pl.BlockSpec(memory_space=pltpu.VMEM)] * (1 + len(pieces)),
        out_specs=pl.BlockSpec(memory_space=pl.ANY),
        scratch_shapes=[
            pltpu.VMEM((nvec, rows, half), F32),
            pltpu.VMEM((nvec, rows, half), B16),
            pltpu.SemaphoreType.DMA((nvec,)),
        ],
        compiler_params=pltpu.CompilerParams(vmem_limit_bytes=24 * 2**20),
        name="arrange",
    )(place, view, *pieces)
    return out.reshape(nvec, share, size * sectors, half)


def general(psi, left_ops, right_ops, shifts, active):
    before, after = neighbours(psi, QMAX)
    padded = jnp.concatenate([before, psi, after], axis=1)
    count = left_ops.shape[0]
    nvec, sectors, blk, _ = psi.shape

    def add_term(index, total):
        source = lax.dynamic_slice_in_dim(padded, QMAX - shifts[index], sectors, 1)
        middle = jnp.einsum("tij,vtjk->vtik", left_ops[index], source, preferred_element_type=F32).astype(B16)
        term = jnp.einsum("vtik,tlk->vlti", middle, right_ops[index], preferred_element_type=F32)
        weight = active[index].astype(F32)
        return total + term * weight[None, None, :, None]

    total = lax.fori_loop(0, count, add_term, jnp.zeros((nvec, blk, sectors, blk), F32))
    summed = lax.psum(total, "op")
    share = blk // lax.axis_size("op")
    owned = lax.dynamic_slice_in_dim(summed, lax.axis_index("op") * share, share, 3)
    return lax.all_to_all(owned.astype(B16), "sec", split_axis=1, concat_axis=2, tiled=True)


def per_device(psi, left_ops, right_ops, shifts, active):
    nvec, sectors, blk, _ = psi.shape
    size, half = lax.axis_size("sec"), blk // 2
    if lax.axis_size("op") != 2 or sectors != 8 or blk % (16 * size) or size % NEAR:
        return general(psi, left_ops, right_ops, shifts, active)
    me = lax.axis_index("op")
    sec = lax.axis_index("sec")
    place = jnp.stack([me, (sec == 0).astype(jnp.int32), (sec == size - 1).astype(jnp.int32), sec // NEAR, sec % NEAR])
    state = (place, shifts, active, psi, left_ops, right_ops)
    early = 3
    first, rest = plan(nvec, sectors, early)
    share, far = blk // size, size // NEAR

    def fence(make, shape, *operands):
        zeros = lambda *_: jax.tree.map(lambda one: jnp.zeros(one.shape, one.dtype), shape)
        return lax.cond(sec < size, make, zeros, *operands)

    def begin(*state):
        mine, theirs = products(first_kernel, early, len(first), *state)
        return blocks(place, mine, swap(theirs), far, NEAR)

    def go_on(*operands):
        *state, halo, earlier = operands
        mine, theirs = products(second_kernel, early, len(rest), *state, halo, swap(halo), earlier)
        return combine([(mine, swap(theirs))], size)

    def near_steps(*parts):
        pieces = [*regroup(parts)]
        for b in range(1, NEAR):
            steps = [(i, i - i % NEAR + (i + b) % NEAR) for i in range(size)]
            pieces[b] = lax.ppermute(pieces[b], "sec", steps)
        return tuple(pieces)

    halo = fetch(psi, me)
    block = jax.ShapeDtypeStruct((NEAR, len(first), share, half), B16)
    parts = [*fence(begin, (block,) * far, *state)]
    for a in range(1, far):
        steps = [(i, (i + a * NEAR) % size) for i in range(size)]
        parts[a] = lax.ppermute(parts[a], "sec", steps)
    block = jax.ShapeDtypeStruct((size, len(rest), share, half), B16)
    owned = after(fence(go_on, block, *state, halo, parts[0]), *parts[1:])
    view = lax.all_to_all(owned, "sec", split_axis=0, concat_axis=0, tiled=True)
    block = jax.ShapeDtypeStruct((far, len(first), share, half), B16)
    pieces = fence(near_steps, (block,) * NEAR, *parts)
    return arrange([first, rest], sectors, nvec, place, view, pieces)


def solution(mesh):
    placed = (
        P(None, "sec", None, None),
        P("op", "sec", None, None),
        P("op", "sec", None, None),
        P("op"),
        P("op", "sec"),
    )
    return jax.shard_map(
        per_device,
        mesh=mesh,
        in_specs=placed,
        out_specs=P(None, "sec", None, "op"),
        check_vma=False,
    )
```

```python
import functools

import jax
import jax.numpy as jnp
from jax import lax
from jax.experimental import pallas as pl
from jax.experimental.pallas import tpu as pltpu
from jax.sharding import PartitionSpec as P

QMAX = 1
NEAR = 4
F32, B16 = jnp.float32, jnp.bfloat16


def neighbours(value, width):
    size, length = lax.axis_size("sec"), value.shape[1]
    up = [(i, i + 1) for i in range(size - 1)]
    down = [(j, i) for i, j in up]
    before = lax.ppermute(lax.slice_in_dim(value, length - width, length, axis=1), "sec", up)
    after = lax.ppermute(lax.slice_in_dim(value, 0, width, axis=1), "sec", down)
    return before, after


def fetch(psi, me):
    size, sectors = lax.axis_size("sec"), psi.shape[1]
    ahead = [(i, i + 1) for i in range(size - 1)]
    back = [(size + j, size + i) for i, j in ahead]
    turns = [(size - 1, 2 * size - 1), (size, 0)]
    part = lax.dynamic_slice_in_dim(psi, (1 - me) * (sectors - QMAX), QMAX, axis=1)
    return lax.ppermute(part, ("op", "sec"), ahead + turns + back)


def swap(value):
    return lax.ppermute(value, "op", [(0, 1), (1, 0)])


def plan(nvec, sectors, early):
    inner = [*range(QMAX, sectors - QMAX)]
    edge = [*range(QMAX), *range(sectors - QMAX, sectors)]
    first, rest = inner[:early], inner[early:] + edge
    return [[(v, t) for t in ts for v in range(nvec)] for ts in (first, rest)]


class Work:
    def __init__(self, refs, psi, left, right, shifts, active, me):
        self.ext, self.lbuf, self.rbuf, self.sem_p, self.sem_l, self.sem_r = refs
        self.psi, self.left, self.right, self.shifts, self.active, self.me = psi, left, right, shifts, active, me
        self.nvec = psi.shape[0]

    def operators(self, t):
        one = pl.ds(t, 1)
        return [
            pltpu.make_async_copy(self.left.at[:, one], self.lbuf.at[:, one], self.sem_l.at[t]),
            pltpu.make_async_copy(self.right.at[:, one], self.rbuf.at[:, one], self.sem_r.at[t]),
        ]

    def source(self, s):
        return pltpu.make_async_copy(self.psi.at[:, pl.ds(s, 1)], self.ext.at[:, pl.ds(s + QMAX, 1)], self.sem_p.at[s])

    def products(self, t, base, mine, theirs):
        count, _, _, blk = self.left.shape
        half = blk // 2
        middles = []
        for k in range(count):
            sources = jnp.concatenate([self.ext[v, t + QMAX - self.shifts[k]] for v in range(self.nvec)], axis=1)
            middle = jnp.dot(self.lbuf[k, t], sources, preferred_element_type=F32)
            middles.append((middle * self.active[k, t].astype(F32)).astype(B16))
        rights = jnp.concatenate([self.rbuf[k, t] for k in range(count)], axis=1)
        stacked = jnp.concatenate(
            [
                jnp.concatenate([m[:, v * blk : (v + 1) * blk] for m in middles], axis=1)
                for v in range(self.nvec)
            ],
            axis=0,
        )
        total = lax.dot_general(stacked, rights, (((1,), (1,)), ((), ())), preferred_element_type=F32).astype(B16)
        for v in range(self.nvec):
            low, high = (total[v * blk + h * half : v * blk + (h + 1) * half] for h in range(2))
            mine[base + v] = jnp.where(self.me == 0, low, high).T
            theirs[base + v] = jnp.where(self.me == 0, high, low).T

    def start(self, first, count):
        for s in range(first - QMAX, first + QMAX):
            self.source(s).start()
        for t in range(first, first + count):
            self.source(t + QMAX).start()
            for copy in self.operators(t):
                copy.start()

    def sector(self, t, base, mine, theirs):
        for copy in self.operators(t):
            copy.wait()
        self.products(t, base, mine, theirs)

    def inner(self, first, count, mine, theirs):
        for s in range(first - QMAX, first + QMAX):
            self.source(s).wait()

        def body(index, carry):
            self.source(first + index + QMAX).wait()
            self.sector(first + index, index * self.nvec, mine, theirs)
            return carry

        lax.fori_loop(0, count, body, 0)


def first_kernel(early, me_ref, shifts, active, psi, left, right, mine, theirs, *refs):
    work = Work(refs, psi, left, right, shifts, active, me_ref[0])
    work.start(QMAX, early)
    work.inner(QMAX, early, mine, theirs)


def second_kernel(early, me_ref, shifts, active, psi, left, right, halo, other, earlier, mine, theirs, *refs):
    nvec, sectors = psi.shape[:2]
    me = me_ref[0]
    *refs, sem_h = refs
    work = Work(refs, psi, left, right, shifts, active, me)
    sides = []
    for index, (source, core) in enumerate(((halo, me), (other, 1 - me))):
        at = core * (sectors + QMAX)
        sides.append(pltpu.make_async_copy(source, work.ext.at[:, pl.ds(at, QMAX)], sem_h.at[index]))
    first, count = QMAX + early, sectors - 2 * QMAX - early
    sides += [work.source(s) for s in range(min(2 * QMAX, first - QMAX))]
    work.start(first, count)
    edge = [*range(QMAX), *range(sectors - QMAX, sectors)]
    for copy in sides:
        copy.start()
    for t in edge:
        for copy in work.operators(t):
            copy.start()
    for s in range(first - QMAX, first + QMAX):
        work.source(s).wait()

    def body(index, carry):
        inner = index < count

        @pl.when(inner)
        def _():
            work.source(first + index + QMAX).wait()

        @pl.when(index == count)
        def _():
            for copy in sides:
                copy.wait()
            for side, at in enumerate((0, sectors + QMAX)):

                @pl.when(me_ref[1 + side] == 1)
                def _(at=at):
                    work.ext[:, at : at + QMAX] = jnp.zeros((nvec, QMAX) + psi.shape[2:], psi.dtype)

        t = jnp.where(inner, first + index, (index - count) * (sectors - QMAX))
        work.sector(t, index * nvec, mine, theirs)
        return carry

    lax.fori_loop(0, count + 2 * QMAX, body, 0)


def products(kernel, early, jobs, me, shifts, active, psi, left, right, *more):
    count, sectors, blk, _ = left.shape
    half = blk // 2
    smem = pl.BlockSpec(memory_space=pltpu.SMEM)
    hbm = pl.BlockSpec(memory_space=pl.ANY)
    out = jax.ShapeDtypeStruct((jobs, blk, half), B16)
    return pl.pallas_call(
        functools.partial(kernel, early),
        out_shape=(out, out),
        in_specs=[smem] * 3 + [hbm] * 3 + [hbm] * len(more),
        out_specs=(pl.BlockSpec(memory_space=pltpu.VMEM),) * 2,
        scratch_shapes=[
            pltpu.VMEM((psi.shape[0], sectors + 2 * QMAX, blk, blk), B16),
            pltpu.VMEM((count, sectors, blk, blk), B16),
            pltpu.VMEM((count, sectors, blk, blk), B16),
            pltpu.SemaphoreType.DMA((sectors,)),
            pltpu.SemaphoreType.DMA((sectors,)),
            pltpu.SemaphoreType.DMA((sectors,)),
        ]
        + ([pltpu.SemaphoreType.DMA((2,))] if more else []),
        compiler_params=pltpu.CompilerParams(vmem_limit_bytes=40 * 2**20),
        cost_estimate=pl.CostEstimate(flops=2 * jobs * 2 * count * blk**3, bytes_accessed=12 * 2**20, transcendentals=0),
        name=kernel.__name__,
    )(me, shifts, active, psi, left, right, *more)


def combine_kernel(parts, behind, *refs):
    pairs, refs = refs[: 2 * parts], refs[2 * parts + behind :]
    owned, (obuf, sem) = refs[0], refs[-2:]
    size, _, share, half = obuf.shape
    base = 0
    for part in range(parts):
        abuf, bbuf = pairs[2 * part], pairs[2 * part + 1]

        def body(job, carry, base=base):
            total = (abuf[job].astype(F32) + bbuf[job].astype(F32)).astype(B16)
            obuf[:, base + job] = total.reshape(size, share, half)
            return carry

        lax.fori_loop(0, abuf.shape[0], body, 0)
        base += abuf.shape[0]
    store = pltpu.make_async_copy(obuf, owned, sem.at[0])
    store.start()
    store.wait()


def after_kernel(value, *refs):
    pass


def after(value, *earlier):
    hbm = pl.BlockSpec(memory_space=pl.ANY)
    return pl.pallas_call(
        after_kernel,
        out_shape=jax.ShapeDtypeStruct(value.shape, value.dtype),
        in_specs=[hbm] * (1 + len(earlier)),
        out_specs=hbm,
        input_output_aliases={0: 0},
        name="after",
    )(value, *earlier)


def combine(pairs, size, *behind):
    refs = [ref for pair in pairs for ref in pair]
    jobs = sum(mine.shape[0] for mine, _ in pairs)
    _, blk, half = refs[0].shape
    hbm = pl.BlockSpec(memory_space=pl.ANY)
    block = (size, jobs, blk // size, half)
    return pl.pallas_call(
        functools.partial(combine_kernel, len(pairs), len(behind)),
        out_shape=jax.ShapeDtypeStruct(block, B16),
        in_specs=[pl.BlockSpec(memory_space=pltpu.VMEM)] * len(refs) + [hbm] * len(behind),
        out_specs=hbm,
        scratch_shapes=[pltpu.VMEM(block, B16), pltpu.SemaphoreType.DMA((1,))],
        compiler_params=pltpu.CompilerParams(vmem_limit_bytes=16 * 2**20),
        cost_estimate=pl.CostEstimate(flops=0, bytes_accessed=0, transcendentals=0),
        name="combine",
    )(*refs, *behind)


def blocks_kernel(place, mine, other, *outs):
    rows_of, near = len(outs), outs[0].shape[0]
    share = outs[0].shape[2]
    z, q = place[3], place[4]
    for a, out in enumerate(outs):

        def body(b, carry, a=a, out=out):
            to = lax.rem(z + a, rows_of) * near + lax.rem(q + b, near)
            rows = pl.ds(pl.multiple_of(to * share, share), share)
            out[b] = (mine[:, rows, :].astype(F32) + other[:, rows, :].astype(F32)).astype(B16)
            return carry

        lax.fori_loop(0, near, body, 0)


def blocks(place, mine, other, far, near):
    jobs, blk, half = mine.shape
    vmem = pl.BlockSpec(memory_space=pltpu.VMEM)
    block = jax.ShapeDtypeStruct((near, jobs, blk // (far * near), half), B16)
    return pl.pallas_call(
        blocks_kernel,
        out_shape=(block,) * far,
        in_specs=[pl.BlockSpec(memory_space=pltpu.SMEM), vmem, vmem],
        out_specs=(vmem,) * far,
        compiler_params=pltpu.CompilerParams(vmem_limit_bytes=16 * 2**20),
        cost_estimate=pl.CostEstimate(flops=0, bytes_accessed=0, transcendentals=0),
        name="blocks",
    )(place, mine, other)


def regroup_kernel(far, *refs):
    for b, out in enumerate(refs[far:]):
        for a in range(far):
            out[a] = refs[a][b]


def regroup(parts):
    near, *block = parts[0].shape
    vmem = pl.BlockSpec(memory_space=pltpu.VMEM)
    out = jax.ShapeDtypeStruct((len(parts), *block), B16)
    return pl.pallas_call(
        functools.partial(regroup_kernel, len(parts)),
        out_shape=(out,) * near,
        in_specs=[vmem] * len(parts),
        out_specs=(vmem,) * near,
        compiler_params=pltpu.CompilerParams(vmem_limit_bytes=16 * 2**20),
        cost_estimate=pl.CostEstimate(flops=16 * 10**9, bytes_accessed=0, transcendentals=0),
        name="regroup",
    )(*parts)


def settle_kernel(jobs, sectors, place, *refs):
    pieces, (out, acc) = refs[:-2], refs[-2:]
    near, (far, _, share, half) = len(pieces), pieces[0].shape
    for a in range(far):
        for b in range(near):
            source = lax.rem(place[3] + far - a, far) * near + lax.rem(place[4] + near - b, near)
            for index, (v, t) in enumerate(jobs):
                rows = pl.ds(source * share * sectors + t, share, stride=sectors)
                acc[v, rows, :] = pieces[b][a, index].astype(F32)
    for v in range(out.shape[0]):
        tiles = acc[v].reshape(far * near, share, sectors, half)
        out[v] = jnp.swapaxes(tiles, 0, 1).reshape(out.shape[1:]).astype(B16)


def settle(jobs, sectors, nvec, place, pieces):
    far, _, share, half = pieces[0].shape
    vmem = pl.BlockSpec(memory_space=pltpu.VMEM)
    return pl.pallas_call(
        functools.partial(settle_kernel, jobs, sectors),
        out_shape=jax.ShapeDtypeStruct((nvec, far * len(pieces) * share * sectors, half), B16),
        in_specs=[pl.BlockSpec(memory_space=pltpu.SMEM)] + [vmem] * len(pieces),
        out_specs=vmem,
        scratch_shapes=[pltpu.VMEM((nvec, far * len(pieces) * share * sectors, half), F32)],
        compiler_params=pltpu.CompilerParams(vmem_limit_bytes=24 * 2**20),
        cost_estimate=pl.CostEstimate(flops=10**9, bytes_accessed=0, transcendentals=0),
        name="settle",
    )(place, *pieces)


def arrange_kernel(jobs, sectors, view, settled, out, acc, obuf, sem):
    size, _, share, half = view.shape
    here = sorted({t for _, t in jobs})
    stores = []
    for vector in range(obuf.shape[0]):

        def body(source, carry, vector=vector):
            for index, (v, t) in enumerate(jobs):
                if v == vector:
                    rows = pl.ds(source * share * sectors + t, share, stride=sectors)
                    acc[vector, rows, :] = view[source, index].astype(F32)
            return carry

        lax.fori_loop(0, size, body, 0, unroll=2)
        tiles = jnp.swapaxes(acc[vector].reshape(size, share, sectors, half), 0, 1)
        before = settled[vector].astype(F32).reshape(tiles.shape)
        row = lax.broadcasted_iota(jnp.int32, tiles.shape, 2)
        direct = functools.reduce(jnp.logical_or, [row == t for t in here])
        obuf[vector] = jnp.where(direct, tiles, before).reshape(obuf.shape[1:]).astype(B16)
        stores.append(pltpu.make_async_copy(obuf.at[vector], out.at[vector], sem.at[vector]))
        stores[-1].start()
    for copy in stores:
        copy.wait()


def arrange(jobs, sectors, view, settled):
    size, _, share, half = view.shape
    nvec, rows, _ = settled.shape
    vmem = pl.BlockSpec(memory_space=pltpu.VMEM)
    out = pl.pallas_call(
        functools.partial(arrange_kernel, jobs, sectors),
        out_shape=jax.ShapeDtypeStruct((nvec, rows, half), B16),
        in_specs=[vmem, vmem],
        out_specs=pl.BlockSpec(memory_space=pl.ANY),
        scratch_shapes=[
            pltpu.VMEM((nvec, rows, half), F32),
            pltpu.VMEM((nvec, rows, half), B16),
            pltpu.SemaphoreType.DMA((nvec,)),
        ],
        compiler_params=pltpu.CompilerParams(vmem_limit_bytes=24 * 2**20),
        name="arrange",
    )(view, settled)
    return out.reshape(nvec, share, size * sectors, half)


def general(psi, left_ops, right_ops, shifts, active):
    before, after = neighbours(psi, QMAX)
    padded = jnp.concatenate([before, psi, after], axis=1)
    count = left_ops.shape[0]
    nvec, sectors, blk, _ = psi.shape

    def add_term(index, total):
        source = lax.dynamic_slice_in_dim(padded, QMAX - shifts[index], sectors, 1)
        middle = jnp.einsum("tij,vtjk->vtik", left_ops[index], source, preferred_element_type=F32).astype(B16)
        term = jnp.einsum("vtik,tlk->vlti", middle, right_ops[index], preferred_element_type=F32)
        weight = active[index].astype(F32)
        return total + term * weight[None, None, :, None]

    total = lax.fori_loop(0, count, add_term, jnp.zeros((nvec, blk, sectors, blk), F32))
    summed = lax.psum(total, "op")
    share = blk // lax.axis_size("op")
    owned = lax.dynamic_slice_in_dim(summed, lax.axis_index("op") * share, share, 3)
    return lax.all_to_all(owned.astype(B16), "sec", split_axis=1, concat_axis=2, tiled=True)


def per_device(psi, left_ops, right_ops, shifts, active):
    nvec, sectors, blk, _ = psi.shape
    size, half = lax.axis_size("sec"), blk // 2
    if lax.axis_size("op") != 2 or sectors != 8 or blk % (16 * size) or size % NEAR:
        return general(psi, left_ops, right_ops, shifts, active)
    me = lax.axis_index("op")
    sec = lax.axis_index("sec")
    place = jnp.stack([me, (sec == 0).astype(jnp.int32), (sec == size - 1).astype(jnp.int32), sec // NEAR, sec % NEAR])
    state = (place, shifts, active, psi, left_ops, right_ops)
    early = 3
    first, rest = plan(nvec, sectors, early)
    share, far = blk // size, size // NEAR

    def fence(make, shape, *operands):
        zeros = lambda *_: jax.tree.map(lambda one: jnp.zeros(one.shape, one.dtype), shape)
        return lax.cond(sec < size, make, zeros, *operands)

    def begin(*state):
        mine, theirs = products(first_kernel, early, len(first), *state)
        return blocks(place, mine, swap(theirs), far, NEAR)

    def go_on(*operands):
        mine, theirs = products(second_kernel, early, len(rest), *operands)
        return combine([(mine, swap(theirs))], size)

    def near_steps(*parts):
        pieces = [*regroup(parts)]
        for b in range(1, NEAR):
            steps = [(i, i - i % NEAR + (i + b) % NEAR) for i in range(size)]
            pieces[b] = lax.ppermute(pieces[b], "sec", steps)
        return tuple(pieces)

    halo = fetch(psi, me)
    block = jax.ShapeDtypeStruct((NEAR, len(first), share, half), B16)
    parts = [*fence(begin, (block,) * far, *state)]
    own = parts[0]
    for a in range(1, far):
        steps = [(i, (i + a * NEAR) % size) for i in range(size)]
        parts[a] = lax.ppermute(parts[a], "sec", steps)
    block = jax.ShapeDtypeStruct((size, len(rest), share, half), B16)
    halo = after(halo, own)
    owned = after(fence(go_on, block, *state, halo, swap(halo), own), *parts[1:])
    view = lax.all_to_all(owned, "sec", split_axis=0, concat_axis=0, tiled=True)
    block = jax.ShapeDtypeStruct((far, len(first), share, half), B16)
    pieces = fence(near_steps, (block,) * NEAR, *parts)
    return arrange(rest, sectors, view, settle(first, sectors, nvec, place, pieces))


def solution(mesh):
    placed = (
        P(None, "sec", None, None),
        P("op", "sec", None, None),
        P("op", "sec", None, None),
        P("op"),
        P("op", "sec"),
    )
    return jax.shard_map(
        per_device,
        mesh=mesh,
        in_specs=placed,
        out_specs=P(None, "sec", None, "op"),
        check_vma=False,
    )
```

```python
import functools

import jax
import jax.numpy as jnp
from jax import lax
from jax.experimental import pallas as pl
from jax.experimental.pallas import tpu as pltpu
from jax.sharding import PartitionSpec as P

QMAX = 1
NEAR = 4
F32, B16 = jnp.float32, jnp.bfloat16


def neighbours(value, width):
    size, length = lax.axis_size("sec"), value.shape[1]
    up = [(i, i + 1) for i in range(size - 1)]
    down = [(j, i) for i, j in up]
    before = lax.ppermute(lax.slice_in_dim(value, length - width, length, axis=1), "sec", up)
    after = lax.ppermute(lax.slice_in_dim(value, 0, width, axis=1), "sec", down)
    return before, after


def fetch(psi, me):
    size, sectors = lax.axis_size("sec"), psi.shape[1]
    ahead = [(i, i + 1) for i in range(size - 1)]
    back = [(size + j, size + i) for i, j in ahead]
    turns = [(size - 1, 2 * size - 1), (size, 0)]
    part = lax.dynamic_slice_in_dim(psi, (1 - me) * (sectors - QMAX), QMAX, axis=1)
    return lax.ppermute(part, ("op", "sec"), ahead + turns + back)


def swap(value):
    return lax.ppermute(value, "op", [(0, 1), (1, 0)])


def plan(nvec, sectors, early):
    inner = [*range(QMAX, sectors - QMAX)]
    edge = [*range(QMAX), *range(sectors - QMAX, sectors)]
    first, rest = inner[:early], inner[early:] + edge
    return [[(v, t) for t in ts for v in range(nvec)] for ts in (first, rest)]


class Work:
    def __init__(self, refs, psi, left, right, shifts, active, me):
        self.ext, self.lbuf, self.rbuf, self.sem_p, self.sem_l, self.sem_r = refs
        self.psi, self.left, self.right, self.shifts, self.active, self.me = psi, left, right, shifts, active, me
        self.nvec = psi.shape[0]

    def operators(self, t):
        one = pl.ds(t, 1)
        return [
            pltpu.make_async_copy(self.left.at[:, one], self.lbuf.at[:, one], self.sem_l.at[t]),
            pltpu.make_async_copy(self.right.at[:, one], self.rbuf.at[:, one], self.sem_r.at[t]),
        ]

    def source(self, s):
        return pltpu.make_async_copy(self.psi.at[:, pl.ds(s, 1)], self.ext.at[:, pl.ds(s + QMAX, 1)], self.sem_p.at[s])

    def products(self, t, base, mine, theirs):
        count, _, _, blk = self.left.shape
        half = blk // 2
        middles = []
        for k in range(count):
            sources = jnp.concatenate([self.ext[v, t + QMAX - self.shifts[k]] for v in range(self.nvec)], axis=1)
            middle = jnp.dot(self.lbuf[k, t], sources, preferred_element_type=F32)
            middles.append((middle * self.active[k, t].astype(F32)).astype(B16))
        rights = jnp.concatenate([self.rbuf[k, t] for k in range(count)], axis=1)
        stacked = jnp.concatenate(
            [
                jnp.concatenate([m[:, v * blk : (v + 1) * blk] for m in middles], axis=1)
                for v in range(self.nvec)
            ],
            axis=0,
        )
        total = lax.dot_general(stacked, rights, (((1,), (1,)), ((), ())), preferred_element_type=F32).astype(B16)
        for v in range(self.nvec):
            low, high = (total[v * blk + h * half : v * blk + (h + 1) * half] for h in range(2))
            mine[base + v] = jnp.where(self.me == 0, low, high).T
            theirs[base + v] = jnp.where(self.me == 0, high, low).T

    def start(self, first, count):
        for s in range(first - QMAX, first + QMAX):
            self.source(s).start()
        for t in range(first, first + count):
            self.source(t + QMAX).start()
            for copy in self.operators(t):
                copy.start()

    def sector(self, t, base, mine, theirs):
        for copy in self.operators(t):
            copy.wait()
        self.products(t, base, mine, theirs)

    def inner(self, first, count, mine, theirs):
        for s in range(first - QMAX, first + QMAX):
            self.source(s).wait()

        def body(index, carry):
            self.source(first + index + QMAX).wait()
            self.sector(first + index, index * self.nvec, mine, theirs)
            return carry

        lax.fori_loop(0, count, body, 0)


def first_kernel(early, me_ref, shifts, active, psi, left, right, mine, theirs, *refs):
    work = Work(refs, psi, left, right, shifts, active, me_ref[0])
    work.start(QMAX, early)
    work.inner(QMAX, early, mine, theirs)


def second_kernel(early, me_ref, shifts, active, psi, left, right, halo, other, earlier, mine, theirs, *refs):
    nvec, sectors = psi.shape[:2]
    me = me_ref[0]
    *refs, sem_h = refs
    work = Work(refs, psi, left, right, shifts, active, me)
    sides = []
    for index, (source, core) in enumerate(((halo, me), (other, 1 - me))):
        at = core * (sectors + QMAX)
        sides.append(pltpu.make_async_copy(source, work.ext.at[:, pl.ds(at, QMAX)], sem_h.at[index]))
    first, count = QMAX + early, sectors - 2 * QMAX - early
    sides += [work.source(s) for s in range(min(2 * QMAX, first - QMAX))]
    work.start(first, count)
    edge = [*range(QMAX), *range(sectors - QMAX, sectors)]
    for copy in sides:
        copy.start()
    for t in edge:
        for copy in work.operators(t):
            copy.start()
    for s in range(first - QMAX, first + QMAX):
        work.source(s).wait()

    def body(index, carry):
        inner = index < count

        @pl.when(inner)
        def _():
            work.source(first + index + QMAX).wait()

        @pl.when(index == count)
        def _():
            for copy in sides:
                copy.wait()
            for side, at in enumerate((0, sectors + QMAX)):

                @pl.when(me_ref[1 + side] == 1)
                def _(at=at):
                    work.ext[:, at : at + QMAX] = jnp.zeros((nvec, QMAX) + psi.shape[2:], psi.dtype)

        t = jnp.where(inner, first + index, (index - count) * (sectors - QMAX))
        work.sector(t, index * nvec, mine, theirs)
        return carry

    lax.fori_loop(0, count + 2 * QMAX, body, 0)


def products(kernel, early, jobs, me, shifts, active, psi, left, right, *more):
    count, sectors, blk, _ = left.shape
    half = blk // 2
    smem = pl.BlockSpec(memory_space=pltpu.SMEM)
    hbm = pl.BlockSpec(memory_space=pl.ANY)
    out = jax.ShapeDtypeStruct((jobs, blk, half), B16)
    return pl.pallas_call(
        functools.partial(kernel, early),
        out_shape=(out, out),
        in_specs=[smem] * 3 + [hbm] * 3 + [hbm] * len(more),
        out_specs=(pl.BlockSpec(memory_space=pltpu.VMEM),) * 2,
        scratch_shapes=[
            pltpu.VMEM((psi.shape[0], sectors + 2 * QMAX, blk, blk), B16),
            pltpu.VMEM((count, sectors, blk, blk), B16),
            pltpu.VMEM((count, sectors, blk, blk), B16),
            pltpu.SemaphoreType.DMA((sectors,)),
            pltpu.SemaphoreType.DMA((sectors,)),
            pltpu.SemaphoreType.DMA((sectors,)),
        ]
        + ([pltpu.SemaphoreType.DMA((2,))] if more else []),
        compiler_params=pltpu.CompilerParams(vmem_limit_bytes=40 * 2**20),
        cost_estimate=pl.CostEstimate(flops=2 * jobs * 2 * count * blk**3, bytes_accessed=12 * 2**20, transcendentals=0),
        name=kernel.__name__,
    )(me, shifts, active, psi, left, right, *more)


def combine_kernel(parts, behind, *refs):
    pairs, refs = refs[: 2 * parts], refs[2 * parts + behind :]
    owned, (obuf, sem) = refs[0], refs[-2:]
    size, _, share, half = obuf.shape
    base = 0
    for part in range(parts):
        abuf, bbuf = pairs[2 * part], pairs[2 * part + 1]

        def body(job, carry, base=base):
            total = (abuf[job].astype(F32) + bbuf[job].astype(F32)).astype(B16)
            obuf[:, base + job] = total.reshape(size, share, half)
            return carry

        lax.fori_loop(0, abuf.shape[0], body, 0)
        base += abuf.shape[0]
    store = pltpu.make_async_copy(obuf, owned, sem.at[0])
    store.start()
    store.wait()


def after_kernel(value, *refs):
    pass


def after(value, *earlier):
    hbm = pl.BlockSpec(memory_space=pl.ANY)
    return pl.pallas_call(
        after_kernel,
        out_shape=jax.ShapeDtypeStruct(value.shape, value.dtype),
        in_specs=[hbm] * (1 + len(earlier)),
        out_specs=hbm,
        input_output_aliases={0: 0},
        name="after",
    )(value, *earlier)


def combine(pairs, size, *behind):
    refs = [ref for pair in pairs for ref in pair]
    jobs = sum(mine.shape[0] for mine, _ in pairs)
    _, blk, half = refs[0].shape
    hbm = pl.BlockSpec(memory_space=pl.ANY)
    block = (size, jobs, blk // size, half)
    return pl.pallas_call(
        functools.partial(combine_kernel, len(pairs), len(behind)),
        out_shape=jax.ShapeDtypeStruct(block, B16),
        in_specs=[pl.BlockSpec(memory_space=pltpu.VMEM)] * len(refs) + [hbm] * len(behind),
        out_specs=hbm,
        scratch_shapes=[pltpu.VMEM(block, B16), pltpu.SemaphoreType.DMA((1,))],
        compiler_params=pltpu.CompilerParams(vmem_limit_bytes=16 * 2**20),
        cost_estimate=pl.CostEstimate(flops=0, bytes_accessed=0, transcendentals=0),
        name="combine",
    )(*refs, *behind)


def blocks_kernel(place, mine, other, *outs):
    rows_of, near = len(outs), outs[0].shape[0]
    share = outs[0].shape[2]
    z, q = place[3], place[4]
    for a, out in enumerate(outs):

        def body(b, carry, a=a, out=out):
            to = lax.rem(z + a, rows_of) * near + lax.rem(q + b, near)
            rows = pl.ds(pl.multiple_of(to * share, share), share)
            out[b] = (mine[:, rows, :].astype(F32) + other[:, rows, :].astype(F32)).astype(B16)
            return carry

        lax.fori_loop(0, near, body, 0)


def blocks(place, mine, other, far, near):
    jobs, blk, half = mine.shape
    vmem = pl.BlockSpec(memory_space=pltpu.VMEM)
    block = jax.ShapeDtypeStruct((near, jobs, blk // (far * near), half), B16)
    return pl.pallas_call(
        blocks_kernel,
        out_shape=(block,) * far,
        in_specs=[pl.BlockSpec(memory_space=pltpu.SMEM), vmem, vmem],
        out_specs=(vmem,) * far,
        compiler_params=pltpu.CompilerParams(vmem_limit_bytes=16 * 2**20),
        cost_estimate=pl.CostEstimate(flops=0, bytes_accessed=0, transcendentals=0),
        name="blocks",
    )(place, mine, other)


def regroup_kernel(far, *refs):
    for b, out in enumerate(refs[far:]):
        for a in range(far):
            out[a] = refs[a][b]


def regroup(parts):
    near, *block = parts[0].shape
    vmem = pl.BlockSpec(memory_space=pltpu.VMEM)
    out = jax.ShapeDtypeStruct((len(parts), *block), B16)
    return pl.pallas_call(
        functools.partial(regroup_kernel, len(parts)),
        out_shape=(out,) * near,
        in_specs=[vmem] * len(parts),
        out_specs=(vmem,) * near,
        compiler_params=pltpu.CompilerParams(vmem_limit_bytes=16 * 2**20),
        cost_estimate=pl.CostEstimate(flops=16 * 10**9, bytes_accessed=0, transcendentals=0),
        name="regroup",
    )(*parts)


def settle_kernel(jobs, sectors, place, *refs):
    pieces, (out, acc) = refs[:-2], refs[-2:]
    near, (far, _, share, half) = len(pieces), pieces[0].shape
    for a in range(far):
        for b in range(near):
            source = lax.rem(place[3] + far - a, far) * near + lax.rem(place[4] + near - b, near)
            for index, (v, t) in enumerate(jobs):
                rows = pl.ds(source * share * sectors + t, share, stride=sectors)
                acc[v, rows, :] = pieces[b][a, index].astype(F32)
    for v in range(out.shape[0]):
        tiles = acc[v, : out.shape[1]].reshape(far * near, share, sectors, half)
        out[v] = jnp.swapaxes(tiles, 0, 1).reshape(out.shape[1:]).astype(B16)


def settle(jobs, sectors, nvec, place, pieces):
    far, _, share, half = pieces[0].shape
    vmem = pl.BlockSpec(memory_space=pltpu.VMEM)
    return pl.pallas_call(
        functools.partial(settle_kernel, jobs, sectors),
        out_shape=jax.ShapeDtypeStruct((nvec, far * len(pieces) * share * sectors, half), B16),
        in_specs=[pl.BlockSpec(memory_space=pltpu.SMEM)] + [vmem] * len(pieces),
        out_specs=vmem,
        scratch_shapes=[pltpu.VMEM((nvec, (far * len(pieces) * share + 1) * sectors, half), F32)],
        compiler_params=pltpu.CompilerParams(vmem_limit_bytes=24 * 2**20),
        cost_estimate=pl.CostEstimate(flops=10**9, bytes_accessed=0, transcendentals=0),
        name="settle",
    )(place, *pieces)


def arrange_kernel(jobs, sectors, view, settled, out, acc, obuf, sem):
    size, _, share, half = view.shape
    here = sorted({t for _, t in jobs})
    stores = []
    for vector in range(obuf.shape[0]):

        def body(source, carry, vector=vector):
            for index, (v, t) in enumerate(jobs):
                if v == vector:
                    rows = pl.ds(source * share * sectors + t, share, stride=sectors)
                    acc[vector, rows, :] = view[source, index].astype(F32)
            return carry

        lax.fori_loop(0, size, body, 0, unroll=2)
        tiles = jnp.swapaxes(acc[vector, : out.shape[1]].reshape(size, share, sectors, half), 0, 1)
        before = settled[vector].astype(F32).reshape(tiles.shape)
        row = lax.broadcasted_iota(jnp.int32, tiles.shape, 2)
        direct = functools.reduce(jnp.logical_or, [row == t for t in here])
        obuf[vector] = jnp.where(direct, tiles, before).reshape(obuf.shape[1:]).astype(B16)
        stores.append(pltpu.make_async_copy(obuf.at[vector], out.at[vector], sem.at[vector]))
        stores[-1].start()
    for copy in stores:
        copy.wait()


def arrange(jobs, sectors, view, settled):
    size, _, share, half = view.shape
    nvec, rows, _ = settled.shape
    vmem = pl.BlockSpec(memory_space=pltpu.VMEM)
    out = pl.pallas_call(
        functools.partial(arrange_kernel, jobs, sectors),
        out_shape=jax.ShapeDtypeStruct((nvec, rows, half), B16),
        in_specs=[vmem, vmem],
        out_specs=pl.BlockSpec(memory_space=pl.ANY),
        scratch_shapes=[
            pltpu.VMEM((nvec, rows + sectors, half), F32),
            pltpu.VMEM((nvec, rows, half), B16),
            pltpu.SemaphoreType.DMA((nvec,)),
        ],
        compiler_params=pltpu.CompilerParams(vmem_limit_bytes=24 * 2**20),
        name="arrange",
    )(view, settled)
    return out.reshape(nvec, share, size * sectors, half)


def general(psi, left_ops, right_ops, shifts, active):
    before, after = neighbours(psi, QMAX)
    padded = jnp.concatenate([before, psi, after], axis=1)
    count = left_ops.shape[0]
    nvec, sectors, blk, _ = psi.shape

    def add_term(index, total):
        source = lax.dynamic_slice_in_dim(padded, QMAX - shifts[index], sectors, 1)
        middle = jnp.einsum("tij,vtjk->vtik", left_ops[index], source, preferred_element_type=F32).astype(B16)
        term = jnp.einsum("vtik,tlk->vlti", middle, right_ops[index], preferred_element_type=F32)
        weight = active[index].astype(F32)
        return total + term * weight[None, None, :, None]

    total = lax.fori_loop(0, count, add_term, jnp.zeros((nvec, blk, sectors, blk), F32))
    summed = lax.psum(total, "op")
    share = blk // lax.axis_size("op")
    owned = lax.dynamic_slice_in_dim(summed, lax.axis_index("op") * share, share, 3)
    return lax.all_to_all(owned.astype(B16), "sec", split_axis=1, concat_axis=2, tiled=True)


def per_device(psi, left_ops, right_ops, shifts, active):
    nvec, sectors, blk, _ = psi.shape
    size, half = lax.axis_size("sec"), blk // 2
    if lax.axis_size("op") != 2 or sectors != 8 or blk % (16 * size) or size % NEAR:
        return general(psi, left_ops, right_ops, shifts, active)
    me = lax.axis_index("op")
    sec = lax.axis_index("sec")
    place = jnp.stack([me, (sec == 0).astype(jnp.int32), (sec == size - 1).astype(jnp.int32), sec // NEAR, sec % NEAR])
    state = (place, shifts, active, psi, left_ops, right_ops)
    early = 3
    first, rest = plan(nvec, sectors, early)
    share, far = blk // size, size // NEAR

    def fence(make, shape, *operands):
        zeros = lambda *_: jax.tree.map(lambda one: jnp.zeros(one.shape, one.dtype), shape)
        return lax.cond(sec < size, make, zeros, *operands)

    def begin(*state):
        mine, theirs = products(first_kernel, early, len(first), *state)
        return blocks(place, mine, swap(theirs), far, NEAR)

    def go_on(*operands):
        mine, theirs = products(second_kernel, early, len(rest), *operands)
        return combine([(mine, swap(theirs))], size)

    def near_steps(*parts):
        pieces = [*regroup(parts)]
        for b in range(1, NEAR):
            steps = [(i, i - i % NEAR + (i + b) % NEAR) for i in range(size)]
            pieces[b] = lax.ppermute(pieces[b], "sec", steps)
        return tuple(pieces)

    halo = fetch(psi, me)
    block = jax.ShapeDtypeStruct((NEAR, len(first), share, half), B16)
    parts = [*fence(begin, (block,) * far, *state)]
    own = parts[0]
    for a in range(1, far):
        steps = [(i, (i + a * NEAR) % size) for i in range(size)]
        parts[a] = lax.ppermute(parts[a], "sec", steps)
    block = jax.ShapeDtypeStruct((size, len(rest), share, half), B16)
    halo = after(halo, own)
    owned = after(fence(go_on, block, *state, halo, swap(halo), own), *parts[1:])
    view = lax.all_to_all(owned, "sec", split_axis=0, concat_axis=0, tiled=True)
    block = jax.ShapeDtypeStruct((far, len(first), share, half), B16)
    pieces = fence(near_steps, (block,) * NEAR, *parts)
    return arrange(rest, sectors, view, settle(first, sectors, nvec, place, pieces))


def solution(mesh):
    placed = (
        P(None, "sec", None, None),
        P("op", "sec", None, None),
        P("op", "sec", None, None),
        P("op"),
        P("op", "sec"),
    )
    return jax.shard_map(
        per_device,
        mesh=mesh,
        in_specs=placed,
        out_specs=P(None, "sec", None, "op"),
        check_vma=False,
    )
```

```python
import functools

import jax
import jax.numpy as jnp
from jax import lax
from jax.experimental import pallas as pl
from jax.experimental.pallas import tpu as pltpu
from jax.sharding import PartitionSpec as P

QMAX = 1
SHARE = 1
NEAR = 4
F32, B16 = jnp.float32, jnp.bfloat16


def neighbours(value, width):
    size, length = lax.axis_size("sec"), value.shape[1]
    up = [(i, i + 1) for i in range(size - 1)]
    down = [(j, i) for i, j in up]
    before = lax.ppermute(lax.slice_in_dim(value, length - width, length, axis=1), "sec", up)
    after = lax.ppermute(lax.slice_in_dim(value, 0, width, axis=1), "sec", down)
    return before, after


def fetch(psi, me):
    size, sectors = lax.axis_size("sec"), psi.shape[1]
    ahead = [(i, i + 1) for i in range(size - 1)]
    back = [(size + j, size + i) for i, j in ahead]
    turns = [(size - 1, 2 * size - 1), (size, 0)]
    part = lax.dynamic_slice_in_dim(psi, (1 - me) * (sectors - QMAX), QMAX, axis=1)
    return lax.ppermute(part, ("op", "sec"), ahead + turns + back)


def swap(value):
    return lax.ppermute(value, "op", [(0, 1), (1, 0)])


def plan(nvec, sectors, early):
    inner = [*range(QMAX, sectors - QMAX)]
    edge = [*range(QMAX), *range(sectors - QMAX, sectors)]
    shared, *later = inner[early:] + edge
    first = [(v, t) for t in inner[:early] for v in range(nvec)] + [(v, shared) for v in range(SHARE)]
    rest = [(v, shared) for v in range(SHARE, nvec)] + [(v, t) for t in later for v in range(nvec)]
    return first, rest


class Work:
    def __init__(self, refs, psi, left, right, shifts, active, me):
        self.ext, self.lbuf, self.rbuf, self.sem_p, self.sem_l, self.sem_r = refs
        self.psi, self.left, self.right, self.shifts, self.active, self.me = psi, left, right, shifts, active, me
        self.nvec = psi.shape[0]

    def operators(self, t):
        one = pl.ds(t, 1)
        return [
            pltpu.make_async_copy(self.left.at[:, one], self.lbuf.at[:, one], self.sem_l.at[t]),
            pltpu.make_async_copy(self.right.at[:, one], self.rbuf.at[:, one], self.sem_r.at[t]),
        ]

    def source(self, s):
        return pltpu.make_async_copy(self.psi.at[:, pl.ds(s, 1)], self.ext.at[:, pl.ds(s + QMAX, 1)], self.sem_p.at[s])

    def products(self, t, base, mine, theirs, vectors):
        count, _, _, blk = self.left.shape
        half = blk // 2
        middles = []
        for k in range(count):
            sources = jnp.concatenate([self.ext[v, t + QMAX - self.shifts[k]] for v in vectors], axis=1)
            middle = jnp.dot(self.lbuf[k, t], sources, preferred_element_type=F32)
            middles.append((middle * self.active[k, t].astype(F32)).astype(B16))
        rights = jnp.concatenate([self.rbuf[k, t] for k in range(count)], axis=1)
        stacked = jnp.concatenate(
            [
                jnp.concatenate([m[:, v * blk : (v + 1) * blk] for m in middles], axis=1)
                for v in range(len(vectors))
            ],
            axis=0,
        )
        total = lax.dot_general(stacked, rights, (((1,), (1,)), ((), ())), preferred_element_type=F32).astype(B16)
        for v in range(len(vectors)):
            low, high = (total[v * blk + h * half : v * blk + (h + 1) * half] for h in range(2))
            mine[base + v] = jnp.where(self.me == 0, low, high).T
            theirs[base + v] = jnp.where(self.me == 0, high, low).T

    def start(self, first, count):
        for s in range(first - QMAX, first + QMAX):
            self.source(s).start()
        for t in range(first, first + count):
            self.source(t + QMAX).start()
            for copy in self.operators(t):
                copy.start()

    def sector(self, t, base, mine, theirs, vectors):
        for copy in self.operators(t):
            copy.wait()
        self.products(t, base, mine, theirs, vectors)

    def inner(self, first, count, mine, theirs):
        for s in range(first - QMAX, first + QMAX):
            self.source(s).wait()

        def body(index, carry):
            self.source(first + index + QMAX).wait()
            self.sector(first + index, index * self.nvec, mine, theirs, range(self.nvec))
            return carry

        lax.fori_loop(0, count, body, 0)


def first_kernel(early, me_ref, shifts, active, psi, left, right, mine, theirs, *refs):
    work = Work(refs, psi, left, right, shifts, active, me_ref[0])
    work.start(QMAX, early + 1)
    work.inner(QMAX, early, mine, theirs)
    shared = QMAX + early
    work.source(shared + QMAX).wait()
    work.sector(shared, early * work.nvec, mine, theirs, range(SHARE))


def second_kernel(early, me_ref, shifts, active, psi, left, right, halo, other, earlier, mine, theirs, *refs):
    nvec, sectors = psi.shape[:2]
    me = me_ref[0]
    *refs, sem_h = refs
    work = Work(refs, psi, left, right, shifts, active, me)
    sides = []
    for index, (source, core) in enumerate(((halo, me), (other, 1 - me))):
        at = core * (sectors + QMAX)
        sides.append(pltpu.make_async_copy(source, work.ext.at[:, pl.ds(at, QMAX)], sem_h.at[index]))
    first, count = QMAX + early, sectors - 2 * QMAX - early
    sides += [work.source(s) for s in range(min(2 * QMAX, first - QMAX))]
    work.start(first, count)
    edge = [*range(QMAX), *range(sectors - QMAX, sectors)]
    for copy in sides:
        copy.start()
    for t in edge:
        for copy in work.operators(t):
            copy.start()
    for s in range(first - QMAX, first + QMAX):
        work.source(s).wait()
    work.source(first + QMAX).wait()
    work.sector(first, 0, mine, theirs, range(SHARE, nvec))
    first, count = first + 1, count - 1

    def body(index, carry):
        inner = index < count

        @pl.when(inner)
        def _():
            work.source(first + index + QMAX).wait()

        @pl.when(index == count)
        def _():
            for copy in sides:
                copy.wait()
            for side, at in enumerate((0, sectors + QMAX)):

                @pl.when(me_ref[1 + side] == 1)
                def _(at=at):
                    work.ext[:, at : at + QMAX] = jnp.zeros((nvec, QMAX) + psi.shape[2:], psi.dtype)

        t = jnp.where(inner, first + index, (index - count) * (sectors - QMAX))
        work.sector(t, index * nvec + nvec - SHARE, mine, theirs, range(nvec))
        return carry

    lax.fori_loop(0, count + 2 * QMAX, body, 0)


def products(kernel, early, jobs, me, shifts, active, psi, left, right, *more):
    count, sectors, blk, _ = left.shape
    half = blk // 2
    smem = pl.BlockSpec(memory_space=pltpu.SMEM)
    hbm = pl.BlockSpec(memory_space=pl.ANY)
    out = jax.ShapeDtypeStruct((jobs, blk, half), B16)
    return pl.pallas_call(
        functools.partial(kernel, early),
        out_shape=(out, out),
        in_specs=[smem] * 3 + [hbm] * 3 + [hbm] * len(more),
        out_specs=(pl.BlockSpec(memory_space=pltpu.VMEM),) * 2,
        scratch_shapes=[
            pltpu.VMEM((psi.shape[0], sectors + 2 * QMAX, blk, blk), B16),
            pltpu.VMEM((count, sectors, blk, blk), B16),
            pltpu.VMEM((count, sectors, blk, blk), B16),
            pltpu.SemaphoreType.DMA((sectors,)),
            pltpu.SemaphoreType.DMA((sectors,)),
            pltpu.SemaphoreType.DMA((sectors,)),
        ]
        + ([pltpu.SemaphoreType.DMA((2,))] if more else []),
        compiler_params=pltpu.CompilerParams(vmem_limit_bytes=40 * 2**20),
        cost_estimate=pl.CostEstimate(flops=2 * jobs * 2 * count * blk**3, bytes_accessed=12 * 2**20, transcendentals=0),
        name=kernel.__name__,
    )(me, shifts, active, psi, left, right, *more)


def combine_kernel(parts, behind, *refs):
    pairs, refs = refs[: 2 * parts], refs[2 * parts + behind :]
    owned, (obuf, sem) = refs[0], refs[-2:]
    size, _, share, half = obuf.shape
    base = 0
    for part in range(parts):
        abuf, bbuf = pairs[2 * part], pairs[2 * part + 1]

        def body(job, carry, base=base):
            total = (abuf[job].astype(F32) + bbuf[job].astype(F32)).astype(B16)
            obuf[:, base + job] = total.reshape(size, share, half)
            return carry

        lax.fori_loop(0, abuf.shape[0], body, 0)
        base += abuf.shape[0]
    store = pltpu.make_async_copy(obuf, owned, sem.at[0])
    store.start()
    store.wait()


def after_kernel(value, *refs):
    pass


def after(value, *earlier):
    hbm = pl.BlockSpec(memory_space=pl.ANY)
    return pl.pallas_call(
        after_kernel,
        out_shape=jax.ShapeDtypeStruct(value.shape, value.dtype),
        in_specs=[hbm] * (1 + len(earlier)),
        out_specs=hbm,
        input_output_aliases={0: 0},
        name="after",
    )(value, *earlier)


def combine(pairs, size, *behind):
    refs = [ref for pair in pairs for ref in pair]
    jobs = sum(mine.shape[0] for mine, _ in pairs)
    _, blk, half = refs[0].shape
    hbm = pl.BlockSpec(memory_space=pl.ANY)
    block = (size, jobs, blk // size, half)
    return pl.pallas_call(
        functools.partial(combine_kernel, len(pairs), len(behind)),
        out_shape=jax.ShapeDtypeStruct(block, B16),
        in_specs=[pl.BlockSpec(memory_space=pltpu.VMEM)] * len(refs) + [hbm] * len(behind),
        out_specs=hbm,
        scratch_shapes=[pltpu.VMEM(block, B16), pltpu.SemaphoreType.DMA((1,))],
        compiler_params=pltpu.CompilerParams(vmem_limit_bytes=16 * 2**20),
        cost_estimate=pl.CostEstimate(flops=0, bytes_accessed=0, transcendentals=0),
        name="combine",
    )(*refs, *behind)


def blocks_kernel(place, mine, other, *outs):
    rows_of, near = len(outs), outs[0].shape[0]
    share = outs[0].shape[2]
    z, q = place[3], place[4]
    for a, out in enumerate(outs):

        def body(b, carry, a=a, out=out):
            to = lax.rem(z + a, rows_of) * near + lax.rem(q + b, near)
            rows = pl.ds(pl.multiple_of(to * share, share), share)
            out[b] = (mine[:, rows, :].astype(F32) + other[:, rows, :].astype(F32)).astype(B16)
            return carry

        lax.fori_loop(0, near, body, 0)


def blocks(place, mine, other, far, near):
    jobs, blk, half = mine.shape
    vmem = pl.BlockSpec(memory_space=pltpu.VMEM)
    block = jax.ShapeDtypeStruct((near, jobs, blk // (far * near), half), B16)
    return pl.pallas_call(
        blocks_kernel,
        out_shape=(block,) * far,
        in_specs=[pl.BlockSpec(memory_space=pltpu.SMEM), vmem, vmem],
        out_specs=(vmem,) * far,
        compiler_params=pltpu.CompilerParams(vmem_limit_bytes=16 * 2**20),
        cost_estimate=pl.CostEstimate(flops=0, bytes_accessed=0, transcendentals=0),
        name="blocks",
    )(place, mine, other)


def regroup_kernel(far, *refs):
    for b, out in enumerate(refs[far:]):
        for a in range(far):
            out[a] = refs[a][b]


def regroup(parts):
    near, *block = parts[0].shape
    vmem = pl.BlockSpec(memory_space=pltpu.VMEM)
    out = jax.ShapeDtypeStruct((len(parts), *block), B16)
    return pl.pallas_call(
        functools.partial(regroup_kernel, len(parts)),
        out_shape=(out,) * near,
        in_specs=[vmem] * len(parts),
        out_specs=(vmem,) * near,
        compiler_params=pltpu.CompilerParams(vmem_limit_bytes=16 * 2**20),
        cost_estimate=pl.CostEstimate(flops=16 * 10**9, bytes_accessed=0, transcendentals=0),
        name="regroup",
    )(*parts)


def settle_kernel(jobs, sectors, place, *refs):
    pieces, (out, acc) = refs[:-2], refs[-2:]
    near, (far, _, share, half) = len(pieces), pieces[0].shape
    for a in range(far):
        for b in range(near):
            source = lax.rem(place[3] + far - a, far) * near + lax.rem(place[4] + near - b, near)
            for index, (v, t) in enumerate(jobs):
                rows = pl.ds(source * share * sectors + t, share, stride=sectors)
                acc[v, rows, :] = pieces[b][a, index].astype(F32)
    for v in range(out.shape[0]):
        tiles = acc[v, : out.shape[1]].reshape(far * near, share, sectors, half)
        out[v] = jnp.swapaxes(tiles, 0, 1).reshape(out.shape[1:]).astype(B16)


def settle(jobs, sectors, nvec, place, pieces):
    far, _, share, half = pieces[0].shape
    vmem = pl.BlockSpec(memory_space=pltpu.VMEM)
    return pl.pallas_call(
        functools.partial(settle_kernel, jobs, sectors),
        out_shape=jax.ShapeDtypeStruct((nvec, far * len(pieces) * share * sectors, half), B16),
        in_specs=[pl.BlockSpec(memory_space=pltpu.SMEM)] + [vmem] * len(pieces),
        out_specs=vmem,
        scratch_shapes=[pltpu.VMEM((nvec, (far * len(pieces) * share + 1) * sectors, half), F32)],
        compiler_params=pltpu.CompilerParams(vmem_limit_bytes=24 * 2**20),
        cost_estimate=pl.CostEstimate(flops=10**9, bytes_accessed=0, transcendentals=0),
        name="settle",
    )(place, *pieces)


def arrange_kernel(jobs, sectors, view, settled, out, acc, obuf, sem):
    size, _, share, half = view.shape
    stores = []
    for vector in range(obuf.shape[0]):

        def body(source, carry, vector=vector):
            for index, (v, t) in enumerate(jobs):
                if v == vector:
                    rows = pl.ds(source * share * sectors + t, share, stride=sectors)
                    acc[vector, rows, :] = view[source, index].astype(F32)
            return carry

        lax.fori_loop(0, size, body, 0, unroll=2)
        tiles = jnp.swapaxes(acc[vector, : out.shape[1]].reshape(size, share, sectors, half), 0, 1)
        before = settled[vector].astype(F32).reshape(tiles.shape)
        here = sorted({t for v, t in jobs if v == vector})
        row = lax.broadcasted_iota(jnp.int32, tiles.shape, 2)
        direct = functools.reduce(jnp.logical_or, [row == t for t in here])
        obuf[vector] = jnp.where(direct, tiles, before).reshape(obuf.shape[1:]).astype(B16)
        stores.append(pltpu.make_async_copy(obuf.at[vector], out.at[vector], sem.at[vector]))
        stores[-1].start()
    for copy in stores:
        copy.wait()


def arrange(jobs, sectors, view, settled):
    size, _, share, half = view.shape
    nvec, rows, _ = settled.shape
    vmem = pl.BlockSpec(memory_space=pltpu.VMEM)
    out = pl.pallas_call(
        functools.partial(arrange_kernel, jobs, sectors),
        out_shape=jax.ShapeDtypeStruct((nvec, rows, half), B16),
        in_specs=[vmem, vmem],
        out_specs=pl.BlockSpec(memory_space=pl.ANY),
        scratch_shapes=[
            pltpu.VMEM((nvec, rows + sectors, half), F32),
            pltpu.VMEM((nvec, rows, half), B16),
            pltpu.SemaphoreType.DMA((nvec,)),
        ],
        compiler_params=pltpu.CompilerParams(vmem_limit_bytes=24 * 2**20),
        name="arrange",
    )(view, settled)
    return out.reshape(nvec, share, size * sectors, half)


def general(psi, left_ops, right_ops, shifts, active):
    before, after = neighbours(psi, QMAX)
    padded = jnp.concatenate([before, psi, after], axis=1)
    count = left_ops.shape[0]
    nvec, sectors, blk, _ = psi.shape

    def add_term(index, total):
        source = lax.dynamic_slice_in_dim(padded, QMAX - shifts[index], sectors, 1)
        middle = jnp.einsum("tij,vtjk->vtik", left_ops[index], source, preferred_element_type=F32).astype(B16)
        term = jnp.einsum("vtik,tlk->vlti", middle, right_ops[index], preferred_element_type=F32)
        weight = active[index].astype(F32)
        return total + term * weight[None, None, :, None]

    total = lax.fori_loop(0, count, add_term, jnp.zeros((nvec, blk, sectors, blk), F32))
    summed = lax.psum(total, "op")
    share = blk // lax.axis_size("op")
    owned = lax.dynamic_slice_in_dim(summed, lax.axis_index("op") * share, share, 3)
    return lax.all_to_all(owned.astype(B16), "sec", split_axis=1, concat_axis=2, tiled=True)


def per_device(psi, left_ops, right_ops, shifts, active):
    nvec, sectors, blk, _ = psi.shape
    size, half = lax.axis_size("sec"), blk // 2
    if lax.axis_size("op") != 2 or sectors != 8 or blk % (16 * size) or size % NEAR:
        return general(psi, left_ops, right_ops, shifts, active)
    me = lax.axis_index("op")
    sec = lax.axis_index("sec")
    place = jnp.stack([me, (sec == 0).astype(jnp.int32), (sec == size - 1).astype(jnp.int32), sec // NEAR, sec % NEAR])
    state = (place, shifts, active, psi, left_ops, right_ops)
    early = 3
    first, rest = plan(nvec, sectors, early)
    share, far = blk // size, size // NEAR

    def fence(make, shape, *operands):
        zeros = lambda *_: jax.tree.map(lambda one: jnp.zeros(one.shape, one.dtype), shape)
        return lax.cond(sec < size, make, zeros, *operands)

    def begin(*state):
        mine, theirs = products(first_kernel, early, len(first), *state)
        return blocks(place, mine, swap(theirs), far, NEAR)

    def go_on(*operands):
        *state, halo, earlier = operands
        mine, theirs = products(second_kernel, early, len(rest), *state, halo, swap(halo), earlier)
        return combine([(mine, swap(theirs))], size)

    def near_steps(*parts):
        pieces = [*regroup(parts)]
        for b in range(1, NEAR):
            steps = [(i, i - i % NEAR + (i + b) % NEAR) for i in range(size)]
            pieces[b] = lax.ppermute(pieces[b], "sec", steps)
        return tuple(pieces)

    halo = fetch(psi, me)
    block = jax.ShapeDtypeStruct((NEAR, len(first), share, half), B16)
    parts = [*fence(begin, (block,) * far, *state)]
    own = parts[0]
    for a in range(1, far):
        steps = [(i, (i + a * NEAR) % size) for i in range(size)]
        parts[a] = lax.ppermute(parts[a], "sec", steps)
    block = jax.ShapeDtypeStruct((size, len(rest), share, half), B16)
    owned = after(fence(go_on, block, *state, halo, own), *parts[1:])
    view = lax.all_to_all(owned, "sec", split_axis=0, concat_axis=0, tiled=True)
    block = jax.ShapeDtypeStruct((far, len(first), share, half), B16)
    pieces = fence(near_steps, (block,) * NEAR, *parts)
    return arrange(rest, sectors, view, settle(first, sectors, nvec, place, pieces))


def solution(mesh):
    placed = (
        P(None, "sec", None, None),
        P("op", "sec", None, None),
        P("op", "sec", None, None),
        P("op"),
        P("op", "sec"),
    )
    return jax.shard_map(
        per_device,
        mesh=mesh,
        in_specs=placed,
        out_specs=P(None, "sec", None, "op"),
        check_vma=False,
    )
```

```python
import functools

import jax
import jax.numpy as jnp
from jax import lax
from jax.experimental import pallas as pl
from jax.experimental.pallas import tpu as pltpu
from jax.sharding import PartitionSpec as P

QMAX = 1
SHARE = 1
NEAR = 4
F32, B16 = jnp.float32, jnp.bfloat16


def neighbours(value, width):
    size, length = lax.axis_size("sec"), value.shape[1]
    up = [(i, i + 1) for i in range(size - 1)]
    down = [(j, i) for i, j in up]
    before = lax.ppermute(lax.slice_in_dim(value, length - width, length, axis=1), "sec", up)
    after = lax.ppermute(lax.slice_in_dim(value, 0, width, axis=1), "sec", down)
    return before, after


def fetch(psi, me):
    size, sectors = lax.axis_size("sec"), psi.shape[1]
    ahead = [(i, i + 1) for i in range(size - 1)]
    back = [(size + j, size + i) for i, j in ahead]
    turns = [(size - 1, 2 * size - 1), (size, 0)]
    part = lax.dynamic_slice_in_dim(psi, (1 - me) * (sectors - QMAX), QMAX, axis=1)
    return lax.ppermute(part, ("op", "sec"), ahead + turns + back)


def swap(value):
    return lax.ppermute(value, "op", [(0, 1), (1, 0)])


def plan(nvec, sectors, early):
    inner = [*range(QMAX, sectors - QMAX)]
    edge = [*range(QMAX), *range(sectors - QMAX, sectors)]
    shared, *later = inner[early:] + edge
    first = [(v, t) for t in inner[:early] for v in range(nvec)] + [(v, shared) for v in range(SHARE)]
    rest = [(v, shared) for v in range(SHARE, nvec)] + [(v, t) for t in later for v in range(nvec)]
    return first, rest


class Work:
    def __init__(self, refs, psi, left, right, shifts, active, me):
        self.ext, self.lbuf, self.rbuf, self.sem_p, self.sem_l, self.sem_r = refs
        self.psi, self.left, self.right, self.shifts, self.active, self.me = psi, left, right, shifts, active, me
        self.nvec = psi.shape[0]

    def operators(self, t):
        one = pl.ds(t, 1)
        return [
            pltpu.make_async_copy(self.left.at[:, one], self.lbuf.at[:, one], self.sem_l.at[t]),
            pltpu.make_async_copy(self.right.at[:, one], self.rbuf.at[:, one], self.sem_r.at[t]),
        ]

    def source(self, s):
        return pltpu.make_async_copy(self.psi.at[:, pl.ds(s, 1)], self.ext.at[:, pl.ds(s + QMAX, 1)], self.sem_p.at[s])

    def products(self, t, base, mine, theirs, vectors):
        count, _, _, blk = self.left.shape
        half = blk // 2
        middles = []
        for k in range(count):
            sources = jnp.concatenate([self.ext[v, t + QMAX - self.shifts[k]] for v in vectors], axis=1)
            middle = jnp.dot(self.lbuf[k, t], sources, preferred_element_type=F32)
            middles.append((middle * self.active[k, t].astype(F32)).astype(B16))
        rights = jnp.concatenate([self.rbuf[k, t] for k in range(count)], axis=1)
        stacked = jnp.concatenate(
            [
                jnp.concatenate([m[:, v * blk : (v + 1) * blk] for m in middles], axis=1)
                for v in range(len(vectors))
            ],
            axis=0,
        )
        total = lax.dot_general(stacked, rights, (((1,), (1,)), ((), ())), preferred_element_type=F32).astype(B16)
        for v in range(len(vectors)):
            low, high = (total[v * blk + h * half : v * blk + (h + 1) * half] for h in range(2))
            mine[base + v] = jnp.where(self.me == 0, low, high).T
            theirs[base + v] = jnp.where(self.me == 0, high, low).T

    def start(self, first, count):
        for s in range(first - QMAX, first + QMAX):
            self.source(s).start()
        for t in range(first, first + count):
            self.source(t + QMAX).start()
            for copy in self.operators(t):
                copy.start()

    def sector(self, t, base, mine, theirs, vectors):
        for copy in self.operators(t):
            copy.wait()
        self.products(t, base, mine, theirs, vectors)

    def inner(self, first, count, mine, theirs):
        for s in range(first - QMAX, first + QMAX):
            self.source(s).wait()

        def body(index, carry):
            self.source(first + index + QMAX).wait()
            self.sector(first + index, index * self.nvec, mine, theirs, range(self.nvec))
            return carry

        lax.fori_loop(0, count, body, 0)


def first_kernel(early, me_ref, shifts, active, psi, left, right, mine, theirs, *refs):
    work = Work(refs, psi, left, right, shifts, active, me_ref[0])
    work.start(QMAX, early + 1)
    work.inner(QMAX, early, mine, theirs)
    shared = QMAX + early
    work.source(shared + QMAX).wait()
    work.sector(shared, early * work.nvec, mine, theirs, range(SHARE))


def second_kernel(early, me_ref, shifts, active, psi, left, right, halo, other, earlier, mine, theirs, *refs):
    nvec, sectors = psi.shape[:2]
    me = me_ref[0]
    *refs, sem_h = refs
    work = Work(refs, psi, left, right, shifts, active, me)
    sides = []
    for index, (source, core) in enumerate(((halo, me), (other, 1 - me))):
        at = core * (sectors + QMAX)
        sides.append(pltpu.make_async_copy(source, work.ext.at[:, pl.ds(at, QMAX)], sem_h.at[index]))
    first, count = QMAX + early, sectors - 2 * QMAX - early
    sides += [work.source(s) for s in range(min(2 * QMAX, first - QMAX))]
    work.start(first, count)
    edge = [*range(QMAX), *range(sectors - QMAX, sectors)]
    for copy in sides:
        copy.start()
    for t in edge:
        for copy in work.operators(t):
            copy.start()
    for s in range(first - QMAX, first + QMAX):
        work.source(s).wait()
    work.source(first + QMAX).wait()
    work.sector(first, 0, mine, theirs, range(SHARE, nvec))
    first, count = first + 1, count - 1

    def body(index, carry):
        inner = index < count

        @pl.when(inner)
        def _():
            work.source(first + index + QMAX).wait()

        @pl.when(index == count)
        def _():
            for copy in sides:
                copy.wait()
            for side, at in enumerate((0, sectors + QMAX)):

                @pl.when(me_ref[1 + side] == 1)
                def _(at=at):
                    work.ext[:, at : at + QMAX] = jnp.zeros((nvec, QMAX) + psi.shape[2:], psi.dtype)

        t = jnp.where(inner, first + index, (index - count) * (sectors - QMAX))
        work.sector(t, index * nvec + nvec - SHARE, mine, theirs, range(nvec))
        return carry

    lax.fori_loop(0, count + 2 * QMAX, body, 0)


def products(kernel, early, jobs, me, shifts, active, psi, left, right, *more):
    count, sectors, blk, _ = left.shape
    half = blk // 2
    smem = pl.BlockSpec(memory_space=pltpu.SMEM)
    hbm = pl.BlockSpec(memory_space=pl.ANY)
    out = jax.ShapeDtypeStruct((jobs, blk, half), B16)
    return pl.pallas_call(
        functools.partial(kernel, early),
        out_shape=(out, out),
        in_specs=[smem] * 3 + [hbm] * 3 + [hbm] * len(more),
        out_specs=(pl.BlockSpec(memory_space=pltpu.VMEM),) * 2,
        scratch_shapes=[
            pltpu.VMEM((psi.shape[0], sectors + 2 * QMAX, blk, blk), B16),
            pltpu.VMEM((count, sectors, blk, blk), B16),
            pltpu.VMEM((count, sectors, blk, blk), B16),
            pltpu.SemaphoreType.DMA((sectors,)),
            pltpu.SemaphoreType.DMA((sectors,)),
            pltpu.SemaphoreType.DMA((sectors,)),
        ]
        + ([pltpu.SemaphoreType.DMA((2,))] if more else []),
        compiler_params=pltpu.CompilerParams(vmem_limit_bytes=40 * 2**20),
        cost_estimate=pl.CostEstimate(flops=2 * jobs * 2 * count * blk**3, bytes_accessed=12 * 2**20, transcendentals=0),
        name=kernel.__name__,
    )(me, shifts, active, psi, left, right, *more)


def combine_kernel(parts, behind, *refs):
    pairs, refs = refs[: 2 * parts], refs[2 * parts + behind :]
    owned, (obuf, sem) = refs[0], refs[-2:]
    size, _, share, half = obuf.shape
    base = 0
    for part in range(parts):
        abuf, bbuf = pairs[2 * part], pairs[2 * part + 1]

        def body(job, carry, base=base):
            total = (abuf[job].astype(F32) + bbuf[job].astype(F32)).astype(B16)
            obuf[:, base + job] = total.reshape(size, share, half)
            return carry

        lax.fori_loop(0, abuf.shape[0], body, 0)
        base += abuf.shape[0]
    store = pltpu.make_async_copy(obuf, owned, sem.at[0])
    store.start()
    store.wait()


def after_kernel(value, *refs):
    pass


def after(value, *earlier):
    hbm = pl.BlockSpec(memory_space=pl.ANY)
    return pl.pallas_call(
        after_kernel,
        out_shape=jax.ShapeDtypeStruct(value.shape, value.dtype),
        in_specs=[hbm] * (1 + len(earlier)),
        out_specs=hbm,
        input_output_aliases={0: 0},
        name="after",
    )(value, *earlier)


def combine(pairs, size, *behind):
    refs = [ref for pair in pairs for ref in pair]
    jobs = sum(mine.shape[0] for mine, _ in pairs)
    _, blk, half = refs[0].shape
    hbm = pl.BlockSpec(memory_space=pl.ANY)
    block = (size, jobs, blk // size, half)
    return pl.pallas_call(
        functools.partial(combine_kernel, len(pairs), len(behind)),
        out_shape=jax.ShapeDtypeStruct(block, B16),
        in_specs=[pl.BlockSpec(memory_space=pltpu.VMEM)] * len(refs) + [hbm] * len(behind),
        out_specs=hbm,
        scratch_shapes=[pltpu.VMEM(block, B16), pltpu.SemaphoreType.DMA((1,))],
        compiler_params=pltpu.CompilerParams(vmem_limit_bytes=16 * 2**20),
        cost_estimate=pl.CostEstimate(flops=0, bytes_accessed=0, transcendentals=0),
        name="combine",
    )(*refs, *behind)


def blocks_kernel(place, mine, other, *outs):
    rows_of, near = len(outs), outs[0].shape[0]
    share = outs[0].shape[2]
    z, q = place[3], place[4]
    for a, out in enumerate(outs):

        for b in range(near):
            to = lax.rem(z + a, rows_of) * near + lax.rem(q + b, near)
            rows = pl.ds(pl.multiple_of(to * share, share), share)
            out[b] = (mine[:, rows, :].astype(F32) + other[:, rows, :].astype(F32)).astype(B16)


def blocks(place, mine, other, far, near):
    jobs, blk, half = mine.shape
    vmem = pl.BlockSpec(memory_space=pltpu.VMEM)
    block = jax.ShapeDtypeStruct((near, jobs, blk // (far * near), half), B16)
    return pl.pallas_call(
        blocks_kernel,
        out_shape=(block,) * far,
        in_specs=[pl.BlockSpec(memory_space=pltpu.SMEM), vmem, vmem],
        out_specs=(vmem,) * far,
        compiler_params=pltpu.CompilerParams(vmem_limit_bytes=16 * 2**20),
        cost_estimate=pl.CostEstimate(flops=0, bytes_accessed=0, transcendentals=0),
        name="blocks",
    )(place, mine, other)


def regroup_kernel(far, *refs):
    for b, out in enumerate(refs[far:]):
        for a in range(far):
            out[a] = refs[a][b]


def regroup(parts):
    near, *block = parts[0].shape
    vmem = pl.BlockSpec(memory_space=pltpu.VMEM)
    out = jax.ShapeDtypeStruct((len(parts), *block), B16)
    return pl.pallas_call(
        functools.partial(regroup_kernel, len(parts)),
        out_shape=(out,) * near,
        in_specs=[vmem] * len(parts),
        out_specs=(vmem,) * near,
        compiler_params=pltpu.CompilerParams(vmem_limit_bytes=16 * 2**20),
        cost_estimate=pl.CostEstimate(flops=16 * 10**9, bytes_accessed=0, transcendentals=0),
        name="regroup",
    )(*parts)


def settle_kernel(jobs, sectors, place, *refs):
    pieces, (out, acc) = refs[:-2], refs[-2:]
    near, (far, _, share, half) = len(pieces), pieces[0].shape
    for a in range(far):
        for b in range(near):
            source = lax.rem(place[3] + far - a, far) * near + lax.rem(place[4] + near - b, near)
            for index, (v, t) in enumerate(jobs):
                rows = pl.ds(source * share * sectors + t, share, stride=sectors)
                acc[v, rows, :] = pieces[b][a, index].astype(F32)
    for v in range(out.shape[0]):
        tiles = acc[v, : out.shape[1]].reshape(far * near, share, sectors, half)
        out[v] = jnp.swapaxes(tiles, 0, 1).reshape(out.shape[1:]).astype(B16)


def settle(jobs, sectors, nvec, place, pieces):
    far, _, share, half = pieces[0].shape
    vmem = pl.BlockSpec(memory_space=pltpu.VMEM)
    return pl.pallas_call(
        functools.partial(settle_kernel, jobs, sectors),
        out_shape=jax.ShapeDtypeStruct((nvec, far * len(pieces) * share * sectors, half), B16),
        in_specs=[pl.BlockSpec(memory_space=pltpu.SMEM)] + [vmem] * len(pieces),
        out_specs=vmem,
        scratch_shapes=[pltpu.VMEM((nvec, (far * len(pieces) * share + 1) * sectors, half), F32)],
        compiler_params=pltpu.CompilerParams(vmem_limit_bytes=24 * 2**20),
        cost_estimate=pl.CostEstimate(flops=10**9, bytes_accessed=0, transcendentals=0),
        name="settle",
    )(place, *pieces)


def arrange_kernel(jobs, sectors, view, settled, out, acc, obuf, sem):
    size, _, share, half = view.shape
    stores = []
    for vector in range(obuf.shape[0]):

        def body(source, carry, vector=vector):
            for index, (v, t) in enumerate(jobs):
                if v == vector:
                    rows = pl.ds(source * share * sectors + t, share, stride=sectors)
                    acc[vector, rows, :] = view[source, index].astype(F32)
            return carry

        lax.fori_loop(0, size, body, 0, unroll=2)
        tiles = jnp.swapaxes(acc[vector, : out.shape[1]].reshape(size, share, sectors, half), 0, 1)
        before = settled[vector].astype(F32).reshape(tiles.shape)
        here = sorted({t for v, t in jobs if v == vector})
        row = lax.broadcasted_iota(jnp.int32, tiles.shape, 2)
        direct = functools.reduce(jnp.logical_or, [row == t for t in here])
        obuf[vector] = jnp.where(direct, tiles, before).reshape(obuf.shape[1:]).astype(B16)
        stores.append(pltpu.make_async_copy(obuf.at[vector], out.at[vector], sem.at[vector]))
        stores[-1].start()
    for copy in stores:
        copy.wait()


def arrange(jobs, sectors, view, settled):
    size, _, share, half = view.shape
    nvec, rows, _ = settled.shape
    vmem = pl.BlockSpec(memory_space=pltpu.VMEM)
    out = pl.pallas_call(
        functools.partial(arrange_kernel, jobs, sectors),
        out_shape=jax.ShapeDtypeStruct((nvec, rows, half), B16),
        in_specs=[vmem, vmem],
        out_specs=pl.BlockSpec(memory_space=pl.ANY),
        scratch_shapes=[
            pltpu.VMEM((nvec, rows + sectors, half), F32),
            pltpu.VMEM((nvec, rows, half), B16),
            pltpu.SemaphoreType.DMA((nvec,)),
        ],
        compiler_params=pltpu.CompilerParams(vmem_limit_bytes=24 * 2**20),
        name="arrange",
    )(view, settled)
    return out.reshape(nvec, share, size * sectors, half)


def general(psi, left_ops, right_ops, shifts, active):
    before, after = neighbours(psi, QMAX)
    padded = jnp.concatenate([before, psi, after], axis=1)
    count = left_ops.shape[0]
    nvec, sectors, blk, _ = psi.shape

    def add_term(index, total):
        source = lax.dynamic_slice_in_dim(padded, QMAX - shifts[index], sectors, 1)
        middle = jnp.einsum("tij,vtjk->vtik", left_ops[index], source, preferred_element_type=F32).astype(B16)
        term = jnp.einsum("vtik,tlk->vlti", middle, right_ops[index], preferred_element_type=F32)
        weight = active[index].astype(F32)
        return total + term * weight[None, None, :, None]

    total = lax.fori_loop(0, count, add_term, jnp.zeros((nvec, blk, sectors, blk), F32))
    summed = lax.psum(total, "op")
    share = blk // lax.axis_size("op")
    owned = lax.dynamic_slice_in_dim(summed, lax.axis_index("op") * share, share, 3)
    return lax.all_to_all(owned.astype(B16), "sec", split_axis=1, concat_axis=2, tiled=True)


def per_device(psi, left_ops, right_ops, shifts, active):
    nvec, sectors, blk, _ = psi.shape
    size, half = lax.axis_size("sec"), blk // 2
    if lax.axis_size("op") != 2 or sectors != 8 or blk % (16 * size) or size % NEAR:
        return general(psi, left_ops, right_ops, shifts, active)
    me = lax.axis_index("op")
    sec = lax.axis_index("sec")
    place = jnp.stack([me, (sec == 0).astype(jnp.int32), (sec == size - 1).astype(jnp.int32), sec // NEAR, sec % NEAR])
    state = (place, shifts, active, psi, left_ops, right_ops)
    early = 3
    first, rest = plan(nvec, sectors, early)
    share, far = blk // size, size // NEAR

    def fence(make, shape, *operands):
        zeros = lambda *_: jax.tree.map(lambda one: jnp.zeros(one.shape, one.dtype), shape)
        return lax.cond(sec < size, make, zeros, *operands)

    def begin(*state):
        mine, theirs = products(first_kernel, early, len(first), *state)
        return blocks(place, mine, swap(theirs), far, NEAR)

    def go_on(*operands):
        *state, halo, earlier = operands
        mine, theirs = products(second_kernel, early, len(rest), *state, halo, swap(halo), earlier)
        return combine([(mine, swap(theirs))], size)

    def near_steps(*parts):
        pieces = [*regroup(parts)]
        for b in range(1, NEAR):
            steps = [(i, i - i % NEAR + (i + b) % NEAR) for i in range(size)]
            pieces[b] = lax.ppermute(pieces[b], "sec", steps)
        return tuple(pieces)

    halo = fetch(psi, me)
    block = jax.ShapeDtypeStruct((NEAR, len(first), share, half), B16)
    parts = [*fence(begin, (block,) * far, *state)]
    own = parts[0]
    for a in range(1, far):
        steps = [(i, (i + a * NEAR) % size) for i in range(size)]
        parts[a] = lax.ppermute(parts[a], "sec", steps)
    block = jax.ShapeDtypeStruct((size, len(rest), share, half), B16)
    owned = after(fence(go_on, block, *state, halo, own), *parts[1:])
    view = lax.all_to_all(owned, "sec", split_axis=0, concat_axis=0, tiled=True)
    block = jax.ShapeDtypeStruct((far, len(first), share, half), B16)
    pieces = fence(near_steps, (block,) * NEAR, *parts)
    return arrange(rest, sectors, view, settle(first, sectors, nvec, place, pieces))


def solution(mesh):
    placed = (
        P(None, "sec", None, None),
        P("op", "sec", None, None),
        P("op", "sec", None, None),
        P("op"),
        P("op", "sec"),
    )
    return jax.shard_map(
        per_device,
        mesh=mesh,
        in_specs=placed,
        out_specs=P(None, "sec", None, "op"),
        check_vma=False,
    )
```
